128 devices in a mesh: task: 4 (over y_hi, core), row: 32 (over x, y_lo, z).
Axes of the slice: x: 4, y: 4 (y_hi: 2, y_lo: 2; y = y_hi * 2 + y_lo), z: 4, core: 2. Of those that a mesh axis runs over, the one named last changes fastest.
Arguments:
- deltas: bfloat16 [8, 25600, 5120], P('task', 'row'), may hold values from -20 to 20, as said below
- sketch: bfloat16 [25600, 128], P('row'), may hold values from -0.0390625 to 0.0390625
Outputs:
- merged: bfloat16 [25600, 5120], P('row', 'task')
The draws below stay inside these ranges and needn't reach their ends.
Inputs may be any that keep to these rules, and one draw needn't show every extreme that they name: Real-valued deltas; the tasks share part of their structure.
All inputs are finite; a program needn't handle non-finite values.
Results may differ from the reference program's by a relative error of at most 0.04.
Values may be sent and summed in bfloat16 or wider, within the bound.
No kernel may reach another device: no remote copies, remote signals or barrier semaphores. Data moves between devices by JAX's collectives and lax.ppermute only.
A program may use at most 128 MiB of HBM per device.

```python
import jax
import jax.numpy as jnp
from jax import lax

D = 5120
FF = 25600
RANK = 128
NS_STEPS = 5
TASKS = 8


def draw_deltas(key, part):
    key = jax.random.fold_in(key, 7)
    shared_key, own_key = jax.random.split(key)
    shared = jax.random.normal(shared_key, (FF, D), jnp.float32)
    own = jax.random.normal(own_key, (TASKS, FF, D), jnp.float32)
    blended = 0.8 * shared[None] + 0.6 * own
    levels = 3.0 ** (jnp.arange(TASKS, dtype=jnp.float32) / (TASKS - 1))
    return jnp.clip(blended * levels[:, None, None], -20.0, 20.0).astype(jnp.bfloat16)


def level_of(key, shape, cuts, least, high):
    factor_of = 1.0
    for axis_at, shards_of in cuts:
        steps = jax.random.uniform(jax.random.fold_in(jax.random.fold_in(key, 6), axis_at), (shards_of,), jnp.float32, least / len(cuts), high / len(cuts))
        factor_of = factor_of * jnp.repeat(jnp.exp(steps), shape[axis_at] // shards_of).reshape((-1,) + (1,) * (len(shape) - 1 - axis_at))
    return factor_of


def gaussian(stream_key, dims, spread, bound, pieces=(), kind=jnp.bfloat16):
    array = spread * jax.random.normal(stream_key, dims, jnp.float32)
    if pieces:
        array = array * level_of(stream_key, dims, pieces, -0.22, 0.18)
    return jnp.clip(array, -bound, bound).astype(kind)


def setup_inputs(seed: int = 0) -> dict:
    streams_of = jax.random.split(jax.random.key(seed), 3)
    deltas = draw_deltas(jax.random.fold_in(streams_of[2], 71), 0)
    sketch = gaussian(streams_of[1], (FF, RANK), FF ** -0.5, 0.0390625, ((0, 32),))
    return {"deltas": deltas, "sketch": sketch}


def reference(deltas, sketch):

    def add_task(carried, delta_task):
        return (carried + delta_task.astype(jnp.float32), None)
    pooled, _ = lax.scan(add_task, jnp.zeros((FF, D), jnp.float32), deltas)

    def sketch_task(carried, delta_task):
        return (carried, jnp.dot(delta_task.T, sketch, preferred_element_type=jnp.float32))
    _, stacked = lax.scan(sketch_task, jnp.zeros((), jnp.float32), deltas)
    basis = jnp.transpose(stacked, (1, 0, 2)).reshape(D, TASKS * RANK).astype(jnp.bfloat16)
    gram = jnp.dot(basis.T, basis, preferred_element_type=jnp.float32)
    frob = jnp.sqrt(jnp.sum(gram * gram))
    identity = jnp.eye(TASKS * RANK, dtype=jnp.float32)
    iterate_y = (gram / frob).astype(jnp.bfloat16)
    iterate_z = identity.astype(jnp.bfloat16)
    for iteration in range(NS_STEPS):
        turn = ((3.0 * identity - jnp.dot(iterate_z, iterate_y, preferred_element_type=jnp.float32)) * 0.5).astype(jnp.bfloat16)
        if iteration == 0:
            iterate_y = jnp.dot(iterate_y, turn, preferred_element_type=jnp.float32).astype(jnp.bfloat16)
        elif iteration + 1 < NS_STEPS:
            iterate_y = jnp.dot(turn, iterate_y, preferred_element_type=jnp.float32).astype(jnp.bfloat16)
        iterate_z = jnp.dot(turn, iterate_z, preferred_element_type=jnp.float32).astype(jnp.bfloat16)
    coeff = (jnp.dot(pooled, basis.astype(jnp.float32), precision=lax.Precision.HIGHEST) / TASKS).astype(jnp.bfloat16)
    second = jnp.dot(coeff, iterate_z, preferred_element_type=jnp.float32).astype(jnp.bfloat16)
    third = (jnp.dot(second, iterate_z, preferred_element_type=jnp.float32) / frob).astype(jnp.bfloat16)
    return jnp.dot(third, basis.T, preferred_element_type=jnp.float32).astype(jnp.bfloat16)
```

```python
import jax
import jax.numpy as jnp
from jax import lax
from jax.experimental import pallas as pl
from jax.experimental.pallas import tpu as pltpu
from jax.sharding import Mesh
from jax.sharding import PartitionSpec as P

NS_STEPS = 5
BF = jnp.bfloat16
F32 = jnp.float32
VMEM_LIMIT = 60 * 1024 * 1024
RING_Y = ("yh", "yl")
SAME_CORE = ("yh", "x", "yl", "z")


def params():
    return pltpu.CompilerParams(vmem_limit_bytes=VMEM_LIMIT)


def whole():
    return pl.BlockSpec(memory_space=pltpu.VMEM)


def shift(value, axis, step):
    size = lax.axis_size(axis)
    return lax.ppermute(value, axis, [(i, (i + step) % size) for i in range(size)])


def sketch_kernel(core_ref, deltas_ref, sketch_ref, out_ref, pool_ref):
    quarter = pl.program_id(0)
    rank = sketch_ref.shape[1]
    for task in range(deltas_ref.shape[0]):
        part = lax.dot_general(
            sketch_ref[...], deltas_ref[task], (((0,), (0,)), ((), ())), preferred_element_type=F32
        )
        rows = part.T.astype(BF)
        rows = rows.reshape(out_ref.shape[1], out_ref.shape[3], rank)
        out_ref[0, :, 0, :, task * rank : (task + 1) * rank] = rows

    @pl.when(quarter % 2 != core_ref[0])
    def _():
        pool_ref[0] = (deltas_ref[0].astype(F32) + deltas_ref[1].astype(F32)).astype(BF)


def sketch_call(core, deltas, sketch):
    tasks, rows, width = deltas.shape
    rank = sketch.shape[1]
    quarter = width // 4
    return pl.pallas_call(
        sketch_kernel,
        grid_spec=pltpu.PrefetchScalarGridSpec(
            num_scalar_prefetch=1,
            grid=(4,),
            in_specs=[
                pl.BlockSpec((tasks, rows, quarter), lambda i, c: (0, 0, i)),
                pl.BlockSpec((rows, rank), lambda i, c: (0, 0)),
            ],
            out_specs=[
                pl.BlockSpec((1, 4, 1, quarter // 4, tasks * rank), lambda i, c: (i // 2, 0, i % 2, 0, 0)),
                pl.BlockSpec((1, rows, quarter), lambda i, c: (i // 2, 0, 0)),
            ],
        ),
        out_shape=[
            jax.ShapeDtypeStruct((2, 4, 2, quarter // 4, tasks * rank), BF),
            jax.ShapeDtypeStruct((2, rows, quarter), BF),
        ],
        compiler_params=params(),
        name="sketch",
    )(core, deltas, sketch)


def gram_kernel(at_ref, a0, a1, a2, a3, a4, b0, b1, b2, b3, b4, basis_ref, gram_ref):
    x, z = at_ref[0], at_ref[1]
    half = a0.shape[3]

    def place(src, own_shift, src_first, count, columns, along_z):
        for j in range(count):
            inner = (0, -1, 1, 2)[src_first + j]
            outer_at = lax.rem((z if along_z else x) + own_shift + 4, 4)
            inner_at = lax.rem((x if along_z else z) + inner + 4, 4)
            xi, zi = (inner_at, outer_at) if along_z else (outer_at, inner_at)
            for h in range(2):
                basis_ref[h, xi, zi, :, columns] = src[j, h]

    for refs, columns, along_z in (
        ((a0, a1, a2, a3, a4), slice(0, half), True),
        ((b0, b1, b2, b3, b4), slice(half, 2 * half), False),
    ):
        place(refs[0], 0, 0, 4, columns, along_z)
        place(refs[1], -1, 0, 4, columns, along_z)
        place(refs[2], 1, 0, 4, columns, along_z)
        place(refs[3], 2, 0, 2, columns, along_z)
        place(refs[4], 2, 2, 2, columns, along_z)

    depth = 2 * 16 * a0.shape[2]
    width = 2 * half
    block = 256
    right = basis_ref[...].reshape(depth, width)
    for i in range(width // block):
        left = basis_ref[:, :, :, :, i * block : (i + 1) * block].reshape(depth, block)
        gram_ref[i * block : (i + 1) * block, :] = lax.dot_general(
            left, right, (((0,), (0,)), ((), ())), preferred_element_type=F32
        ).astype(BF)


def gram_call(at, parts):
    _, _, rows, half = parts[0].shape
    return pl.pallas_call(
        gram_kernel,
        in_specs=[pl.BlockSpec(memory_space=pltpu.SMEM)] + [whole()] * 10,
        out_specs=[whole(), whole()],
        out_shape=[
            jax.ShapeDtypeStruct((2, 4, 4, rows, 2 * half), BF),
            jax.ShapeDtypeStruct((2 * half, 2 * half), BF),
        ],
        compiler_params=params(),
        name="gram",
    )(at, *parts)


def coeff_kernel(core_ref, deltas_ref, pool_ref, basis_ref, out_ref, acc_ref):
    step = pl.program_id(0)
    pooled = (
        deltas_ref[0].astype(F32) + deltas_ref[1].astype(F32) + pool_ref[0].astype(F32)
    ).astype(BF)
    part = jnp.dot(pooled, basis_ref[0], preferred_element_type=F32)

    @pl.when(step == 0)
    def _():
        acc_ref[...] = part

    @pl.when(step == 1)
    def _():
        out_ref[...] = (acc_ref[...] + part).astype(BF)


def coeff_call(core, deltas, pool, basis):
    tasks, rows, width = deltas.shape
    quarter = width // 4
    columns = basis.shape[2]
    return pl.pallas_call(
        coeff_kernel,
        grid_spec=pltpu.PrefetchScalarGridSpec(
            num_scalar_prefetch=1,
            grid=(2,),
            in_specs=[
                pl.BlockSpec((tasks, rows, quarter), lambda i, c: (0, 0, 2 * i + c[0])),
                pl.BlockSpec((1, rows, quarter), lambda i, c: (i, 0, 0)),
                pl.BlockSpec((1, quarter, columns), lambda i, c: (i, 0, 0)),
            ],
            out_specs=pl.BlockSpec((rows, columns), lambda i, c: (0, 0)),
            scratch_shapes=[pltpu.VMEM((rows, columns), F32)],
        ),
        out_shape=jax.ShapeDtypeStruct((rows, columns), BF),
        compiler_params=params(),
        name="coeff",
    )(core, deltas, pool, basis)


def schulz_kernel(own_ref, other_ref, z_ref, frob_ref, y_ref, t_ref, y2_ref, z2_ref):
    size = own_ref.shape[0]
    block = 256
    blocks = size // block

    total = jnp.zeros((8, size), F32)
    for i in range(blocks):
        rows = slice(i * block, (i + 1) * block)
        gram = own_ref[rows, :].astype(F32) + other_ref[rows, :].astype(F32)
        total = total + jnp.sum((gram * gram).reshape(block // 8, 8, size), axis=0)
    frob = jnp.sqrt(jnp.sum(total, keepdims=True))
    frob_ref[...] = jnp.broadcast_to(frob, frob_ref.shape)

    def turn_of(value, first_row, first_col):
        row = lax.broadcasted_iota(jnp.int32, value.shape, 0) + first_row
        col = lax.broadcasted_iota(jnp.int32, value.shape, 1) + first_col
        return ((jnp.where(row == col, 3.0, 0.0) - value) * 0.5).astype(BF)

    for i in range(blocks):
        rows = slice(i * block, (i + 1) * block)
        gram = own_ref[rows, :].astype(F32) + other_ref[rows, :].astype(F32)
        y = (gram / frob).astype(BF)
        y_ref[rows, :] = y
        t_ref[rows, :] = turn_of(y.astype(F32), i * block, 0)

    def product(left, right, out, turn):
        @pl.loop(0, blocks)
        def _(j):
            columns = pl.ds(pl.multiple_of(j * block, block), block)
            value = jnp.dot(left[...], right[:, columns], preferred_element_type=F32)
            out[:, columns] = turn_of(value, 0, j * block) if turn else value.astype(BF)

    product(y_ref, t_ref, y2_ref, False)
    z2_ref[...] = t_ref[...]
    y_now, z_now, y_next, z_next = y2_ref, z2_ref, y_ref, z_ref
    for iteration in range(1, NS_STEPS):
        product(z_now, y_now, t_ref, True)
        if iteration + 1 < NS_STEPS:
            product(t_ref, y_now, y_next, False)
        product(t_ref, z_now, z_next, False)
        y_now, y_next = y_next, y_now
        z_now, z_next = z_next, z_now
    if z_now is not z_ref:
        z_ref[...] = z_now[...]


def schulz_call(own, other):
    size = own.shape[0]
    square = (size, size)
    return pl.pallas_call(
        schulz_kernel,
        in_specs=[whole(), whole()],
        out_specs=[whole(), whole()],
        out_shape=[jax.ShapeDtypeStruct(square, BF), jax.ShapeDtypeStruct((8, 128), F32)],
        scratch_shapes=[pltpu.VMEM(square, BF)] * 4,
        cost_estimate=pl.CostEstimate(flops=24 * size**3, bytes_accessed=6 * size**2, transcendentals=0),
        compiler_params=params(),
        name="schulz",
    )(own, other)


def merge_kernel(coeff_ref, z_ref, frob_ref, basis_ref, out_ref):
    second = jnp.dot(coeff_ref[...], z_ref[...], preferred_element_type=F32).astype(BF)
    third = jnp.dot(second, z_ref[...], preferred_element_type=F32)
    third = (third / frob_ref[0:1, 0:1]).astype(BF)
    out_ref[...] = lax.dot_general(
        third, basis_ref[0], (((1,), (1,)), ((), ())), preferred_element_type=F32
    ).astype(BF)


def merge_call(yh, coeff, z, frob, basis):
    rows, width = coeff.shape
    columns = basis.shape[1]
    block = rows // 2
    return pl.pallas_call(
        lambda at, *refs: merge_kernel(*refs),
        grid_spec=pltpu.PrefetchScalarGridSpec(
            num_scalar_prefetch=1,
            grid=(2,),
            in_specs=[
                pl.BlockSpec((block, width), lambda i, h: (i, 0)),
                pl.BlockSpec((width, width), lambda i, h: (0, 0)),
                pl.BlockSpec((8, 128), lambda i, h: (0, 0)),
                pl.BlockSpec((1, columns, width), lambda i, h: (h[0], 0, 0)),
            ],
            out_specs=pl.BlockSpec((block, columns), lambda i, h: (i, 0)),
        ),
        out_shape=jax.ShapeDtypeStruct((rows, columns), BF),
        compiler_params=params(),
        name="merge",
    )(yh, coeff, z, frob, basis)


def ring_gather(items):
    first = [(shift(a, axis, 1), shift(a, axis, -1)) for a, axis in items]
    out = []
    for (a, axis), (before, after) in zip(items, first):
        cut = a.shape[0] // 2
        low = shift(before[:cut], axis, 1)
        high = shift(after[cut:], axis, -1)
        out.append((a, before, after, low, high))
    return out


def body(deltas, sketch):
    tasks, rows, width = deltas.shape
    core, yh, yl = lax.axis_index("core"), lax.axis_index("yh"), lax.axis_index("yl")
    x, z = lax.axis_index("x"), lax.axis_index("z")
    core1 = core.astype(jnp.int32).reshape(1)

    terms, pool_out = sketch_call(core1, deltas, sketch)
    pool_in = shift(pool_out, "core", 1)

    chips = 64
    piece = width // chips
    group_width = terms.shape[-1]
    arrived = lax.all_to_all(
        terms.reshape(chips, piece, group_width), SAME_CORE, 0, 0, tiled=True
    )
    summed = jnp.sum(arrived.reshape(2, chips // 2, piece, group_width).astype(F32), axis=1).astype(BF)
    own = jnp.concatenate([summed[0], summed[1]], axis=1)

    below, above, across = shift(own, RING_Y, 1), shift(own, RING_Y, -1), shift(own, RING_Y, 2)
    near = jnp.where(yl == 0, above, below)
    far = jnp.where(yl == 0, below, above)
    low_first = yh == 0
    same = jnp.stack([jnp.where(low_first, own, across), jnp.where(low_first, across, own)])
    other = jnp.stack([jnp.where(low_first, near, far), jnp.where(low_first, far, near)])
    keep = jnp.where(yl == core, same, other)
    give = jnp.where(yl == core, other, same)
    got = shift(give, "core", 1)
    part_a = jnp.where(core == 0, keep, got)
    part_b = jnp.where(core == 0, got, keep)

    mid = ring_gather([(part_a, "x"), (part_b, "z")])
    stacked = [
        jnp.stack([m[0], m[1], m[2], jnp.concatenate([m[3], m[4]], axis=0)]) for m in mid
    ]
    last = ring_gather([(stacked[0], "z"), (stacked[1], "x")])
    at = jnp.stack([x, z]).astype(jnp.int32)
    basis, gram_own = gram_call(at, [*last[0], *last[1]])
    basis = basis.reshape(2, width // 4, basis.shape[-1])

    gram_other = shift(gram_own, "core", 1)
    coeff_part = coeff_call(core1, deltas, pool_in, basis)

    half = rows // 2
    mine = lax.dynamic_slice_in_dim(coeff_part, core * half, half, 0)
    give = lax.dynamic_slice_in_dim(coeff_part, (1 - core) * half, half, 0)
    chip_sum = (mine.astype(F32) + shift(give, "core", 1).astype(F32)).astype(BF)
    over = shift(chip_sum, "yh", 1)
    total_tasks = tasks * lax.axis_size("yh") * lax.axis_size("core")
    coeff_half = ((chip_sum.astype(F32) + over.astype(F32)) / total_tasks).astype(BF)
    coeff_twin = shift(coeff_half, "core", 1)
    coeff = jnp.concatenate(
        [jnp.where(core == 0, coeff_half, coeff_twin), jnp.where(core == 0, coeff_twin, coeff_half)]
    )

    inverse_root, frob = schulz_call(gram_own, gram_other)
    return merge_call(yh.astype(jnp.int32).reshape(1), coeff, inverse_root, frob, basis)


def solution(mesh):
    fine = Mesh(mesh.devices.reshape(2, 2, 4, 2, 4), ("yh", "core", "x", "yl", "z"))
    task, row = ("yh", "core"), ("x", "yl", "z")
    return jax.shard_map(
        body,
        mesh=fine,
        in_specs=(P(task, row, None), P(row, None)),
        out_specs=P(row, task),
        check_vma=False,
    )
```

```python
import functools

import jax
import jax.numpy as jnp
from jax import lax
from jax.experimental import pallas as pl
from jax.experimental.pallas import tpu as pltpu
from jax.sharding import Mesh
from jax.sharding import PartitionSpec as P

NS_STEPS = 5
BF = jnp.bfloat16
F32 = jnp.float32
NS_BLOCK = 256
GRAM_BLOCK = 256
MIB = 1024 * 1024
RING_Y = ("yh", "yl")


def params(mib=24):
    return pltpu.CompilerParams(vmem_limit_bytes=mib * MIB)


def whole():
    return pl.BlockSpec(memory_space=pltpu.VMEM)


def shift(value, axis, step):
    size = lax.axis_size(axis)
    return lax.ppermute(value, axis, [(i, (i + step) % size) for i in range(size)])


def sketch_kernel(at_ref, deltas_ref, sketch_ref, *rest):
    outs, keep_ref, give_ref, rows_ref = rest[:10], rest[10], rest[11], rest[12]
    quarter = pl.program_id(0)
    rank = sketch_ref.shape[1]
    piece = rows_ref.shape[2]
    x, z = at_ref[0], at_ref[1]
    for task in range(2):
        part = lax.dot_general(
            sketch_ref[...], deltas_ref[task], (((0,), (0,)), ((), ())), preferred_element_type=F32
        )
        rows_ref[...] = part.astype(BF).T.reshape(4, 4, piece, rank)
        own, up, down, low, high = outs[5 * task : 5 * task + 5]
        for d in range(4):
            for e in range(4):
                over_x, over_z = (d, e) if task == 0 else (e, d)
                value = rows_ref[lax.rem(x + over_x, 4), lax.rem(z + over_z, 4)]
                if d == 2:
                    (low if e < 2 else high)[e % 2, quarter] = value
                else:
                    (own, up, None, down)[d][e, quarter] = value

    total = deltas_ref[0] + deltas_ref[1]
    mine = quarter % 2 == at_ref[3]

    @pl.when(mine)
    def _():
        keep_ref[0] = total

    @pl.when(jnp.logical_not(mine))
    def _():
        give_ref[0] = total


def sketch_call(at, deltas, sketch):
    tasks, rows, width = deltas.shape
    rank = sketch.shape[1]
    quarter = width // 4
    full, half = (4, 4, quarter // 16, rank), (2, 4, quarter // 16, rank)
    shapes = [full, full, full, half, half] * 2
    return pl.pallas_call(
        sketch_kernel,
        grid_spec=pltpu.PrefetchScalarGridSpec(
            num_scalar_prefetch=1,
            grid=(4,),
            in_specs=[
                pl.BlockSpec((tasks, rows, quarter), lambda i, at: (0, 0, i)),
                pl.BlockSpec((rows, rank), lambda i, at: (0, 0)),
            ],
            out_specs=[pl.BlockSpec(shape, lambda i, at: (0, 0, 0, 0)) for shape in shapes]
            + [pl.BlockSpec((1, rows, quarter), lambda i, at: (i // 2, 0, 0))] * 2,
            scratch_shapes=[pltpu.VMEM(full, BF)],
        ),
        out_shape=[jax.ShapeDtypeStruct(shape, BF) for shape in shapes]
        + [jax.ShapeDtypeStruct((2, rows, quarter), BF)] * 2,
        compiler_params=params(48),
        name="sketch",
    )(at, deltas, sketch)


def upper_blocks(size, block):
    return [(slice(i, i + block), slice(i, size)) for i in range(0, size, block)]


def mirror(out, rows, value, block):
    first = rows.start
    out[rows, first:] = value
    for j in range(block, value.shape[1], block):
        out[first + j : first + j + block, rows] = value[:, j : j + block].T


def pack_rows(refs, packed_ref):
    at = 0
    for ref in refs:
        count, rows, width = ref.shape
        packed_ref[at : at + count * rows, :] = ref[...].reshape(count * rows, width)
        at += count * rows


def place_rows(at_ref, blocks, basis_ref):
    x, z = at_ref[0], at_ref[1]
    for ref, chunk, outer, first in blocks:
        for j in range(ref.shape[0]):
            inner = (0, -1, 1, 2)[first + j]
            over_x, over_z = (inner, outer) if chunk == 0 else (outer, inner)
            basis_ref[chunk, lax.rem(x + over_x + 4, 4), lax.rem(z + over_z + 4, 4)] = ref[j]


def gram_first_kernel(at_ref, a0, a1, a2, b0, b1, b2, acc_ref, basis_ref, packed_ref):
    pack_rows([a0, a1, a2, b0, b1, b2], packed_ref)
    for rows, columns in upper_blocks(acc_ref.shape[0], GRAM_BLOCK):
        acc_ref[rows, columns] = lax.dot_general(
            packed_ref[:, rows], packed_ref[:, columns], (((0,), (0,)), ((), ())), preferred_element_type=F32
        )
    near = [(a0, 0, 0, 0), (a1, 0, -1, 0), (a2, 0, 1, 0), (b0, 1, 0, 0), (b1, 1, -1, 0), (b2, 1, 1, 0)]
    place_rows(at_ref, near, basis_ref)


def gram_first_call(at, parts):
    count, rows, width = parts[0].shape
    return pl.pallas_call(
        gram_first_kernel,
        in_specs=[pl.BlockSpec(memory_space=pltpu.SMEM)] + [whole()] * 6,
        out_specs=[whole()] * 2,
        out_shape=[
            jax.ShapeDtypeStruct((width, width), F32),
            jax.ShapeDtypeStruct((2, 4, 4, rows, width), BF),
        ],
        scratch_shapes=[pltpu.VMEM((6 * count * rows, width), BF)],
        cost_estimate=pl.CostEstimate(
            flops=8 * count * rows * width * width, bytes_accessed=8 * count * rows * width, transcendentals=0
        ),
        compiler_params=params(24),
        name="gram_first",
    )(at, *parts)


def gram_last_kernel(at_ref, a3, a4, b3, b4, acc_ref, near_ref, gram_ref, basis_ref, packed_ref):
    pack_rows([a3, a4, b3, b4], packed_ref)
    for rows, columns in upper_blocks(acc_ref.shape[0], GRAM_BLOCK):
        value = lax.dot_general(
            packed_ref[:, rows], packed_ref[:, columns], (((0,), (0,)), ((), ())), preferred_element_type=F32
        )
        mirror(gram_ref, rows, (acc_ref[rows, columns] + value).astype(BF), GRAM_BLOCK)
    basis_ref[...] = near_ref[...]
    place_rows(at_ref, [(a3, 0, 2, 0), (a4, 0, 2, 2), (b3, 1, 2, 0), (b4, 1, 2, 2)], basis_ref)


def gram_last_call(at, parts, acc, near):
    count, rows, width = parts[0].shape
    return pl.pallas_call(
        gram_last_kernel,
        in_specs=[pl.BlockSpec(memory_space=pltpu.SMEM)] + [whole()] * 6,
        out_specs=[whole()] * 2,
        out_shape=[
            jax.ShapeDtypeStruct((width, width), BF),
            jax.ShapeDtypeStruct(near.shape, BF),
        ],
        scratch_shapes=[pltpu.VMEM((4 * count * rows, width), BF)],
        compiler_params=params(24),
        name="gram_last",
    )(at, *parts, acc, near)


def coeff_kernel(at_ref, basis_ref, pool0_ref, pool1_ref, keep_ref, give_ref, chunk_ref):
    chunk_ref[...] = basis_ref[at_ref[2]]
    half, width = keep_ref.shape
    block = 256
    for out_ref, which in ((give_ref, 1 - at_ref[3]), (keep_ref, at_ref[3])):
        rows = pl.ds(pl.multiple_of(which * half, 16), half)
        for i in range(0, width, block):
            columns = slice(i, i + block)
            value = jnp.dot(pool0_ref[rows, :], basis_ref[0, :, columns], preferred_element_type=F32)
            value = value + jnp.dot(pool1_ref[rows, :], basis_ref[1, :, columns], preferred_element_type=F32)
            out_ref[:, columns] = value.astype(BF)


def coeff_call(at, basis, pooled):
    _, depth, width = basis.shape
    rows = pooled[0].shape[0]
    half = jax.ShapeDtypeStruct((rows // 2, width), BF)
    return pl.pallas_call(
        coeff_kernel,
        in_specs=[pl.BlockSpec(memory_space=pltpu.SMEM)] + [whole()] * 3,
        out_specs=[whole()] * 3,
        out_shape=[half, half, jax.ShapeDtypeStruct((depth, width), BF)],
        cost_estimate=pl.CostEstimate(
            flops=4 * rows * depth * width, bytes_accessed=4 * rows * depth, transcendentals=0
        ),
        compiler_params=params(20),
        name="coeff",
    )(at, basis, *pooled)


def turn_of(value, first_row, first_col):
    row = lax.broadcasted_iota(jnp.int32, value.shape, 0) + first_row
    col = lax.broadcasted_iota(jnp.int32, value.shape, 1) + first_col
    return ((jnp.where(row == col, 3.0, 0.0) - value) * 0.5).astype(BF)


def product(left, right, out, turn):
    for rows, columns in upper_blocks(left.shape[0], NS_BLOCK):
        value = jnp.dot(left[rows, :], right[:, columns], preferred_element_type=F32)
        value = turn_of(value, rows.start, columns.start) if turn else value.astype(BF)
        mirror(out, rows, value, NS_BLOCK)


def first_kernel(own_ref, other_ref, y_ref, t_ref, frob_ref, gram_ref):
    size = own_ref.shape[0]
    total = jnp.zeros((8, size), F32)
    for i in range(0, size, NS_BLOCK):
        rows = slice(i, i + NS_BLOCK)
        gram = own_ref[rows, :].astype(F32) + other_ref[rows, :].astype(F32)
        gram_ref[rows, :] = gram
        total = total + jnp.sum((gram * gram).reshape(NS_BLOCK // 8, 8, size), axis=0)
    frob = jnp.sqrt(jnp.sum(total, keepdims=True))
    frob_ref[...] = jnp.broadcast_to(frob, frob_ref.shape)
    scale = 1.0 / frob
    for i in range(0, size, NS_BLOCK):
        rows = slice(i, i + NS_BLOCK)
        y = (gram_ref[rows, :] * scale).astype(BF)
        y_ref[rows, :] = y
        t_ref[rows, :] = turn_of(y.astype(F32), i, 0)


def first_call(own, other):
    square = jax.ShapeDtypeStruct(own.shape, BF)
    return pl.pallas_call(
        first_kernel,
        in_specs=[whole()] * 2,
        out_specs=[whole()] * 3,
        out_shape=[square, square, jax.ShapeDtypeStruct((8, 128), F32)],
        scratch_shapes=[pltpu.VMEM(own.shape, F32)],
        cost_estimate=pl.CostEstimate(flops=16 * own.size, bytes_accessed=8 * own.size, transcendentals=0),
        compiler_params=params(20),
        name="schulz_first",
    )(own, other)


def rest_kernel(y_ref, z_ref, chunk_ref, out_ref, turned_ref, t_ref, ya_ref, za_ref, yb_ref):
    product(y_ref, z_ref, yb_ref, False)
    product(z_ref, yb_ref, t_ref, True)
    product(t_ref, yb_ref, ya_ref, False)
    product(t_ref, z_ref, za_ref, False)
    product(za_ref, ya_ref, t_ref, True)
    product(t_ref, ya_ref, yb_ref, False)
    product(t_ref, za_ref, out_ref, False)
    product(out_ref, yb_ref, t_ref, True)
    product(t_ref, yb_ref, ya_ref, False)
    product(t_ref, out_ref, za_ref, False)
    product(za_ref, ya_ref, t_ref, True)
    product(t_ref, za_ref, out_ref, False)
    for i in range(0, chunk_ref.shape[0], NS_BLOCK):
        turned_ref[:, i : i + NS_BLOCK] = chunk_ref[i : i + NS_BLOCK, :].T


def rest_call(y, z, chunk):
    assert NS_STEPS == 5
    return pl.pallas_call(
        rest_kernel,
        in_specs=[whole()] * 3,
        out_specs=[whole()] * 2,
        out_shape=[
            jax.ShapeDtypeStruct(y.shape, BF),
            jax.ShapeDtypeStruct(chunk.shape[::-1], BF),
        ],
        scratch_shapes=[pltpu.VMEM(y.shape, BF)] * 4,
        cost_estimate=pl.CostEstimate(
            flops=24 * y.size * y.shape[0], bytes_accessed=6 * y.size, transcendentals=0
        ),
        compiler_params=params(24),
        name="schulz_rest",
    )(y, z, chunk)


def third_kernel(coeff_ref, z_ref, frob_ref, out_ref):
    second = jnp.dot(coeff_ref[...], z_ref[...], preferred_element_type=F32).astype(BF)
    third = jnp.dot(second, z_ref[...], preferred_element_type=F32)
    out_ref[...] = (third / frob_ref[0:1, 0:1]).astype(BF)


def third_call(coeff, z, frob):
    return pl.pallas_call(
        third_kernel,
        in_specs=[whole()] * 3,
        out_specs=whole(),
        out_shape=jax.ShapeDtypeStruct(coeff.shape, BF),
        compiler_params=params(),
        name="third",
    )(coeff, z, frob)


def merge_kernel(at_ref, third_ref, chunk_ref, *rest):
    out_ref = rest[-1]
    out_ref[...] = jnp.dot(third_ref[...], chunk_ref[...], preferred_element_type=F32).astype(BF)


def merge_call(at, third, chunk, so_far):
    rows, width = third.shape
    columns = chunk.shape[1]
    in_specs = [
        pl.BlockSpec((rows, width), lambda i, at: (0, 0)),
        pl.BlockSpec((width, columns), lambda i, at: (0, 0)),
    ]
    operands = [at, third, chunk]
    if so_far is None:
        place = lambda i, at: (at[3], 0)
    else:
        place = lambda i, at: (1 - at[3], 0)
        in_specs.append(pl.BlockSpec(memory_space=pl.ANY))
        operands.append(so_far)
    return pl.pallas_call(
        merge_kernel,
        grid_spec=pltpu.PrefetchScalarGridSpec(
            num_scalar_prefetch=1,
            grid=(1,),
            in_specs=in_specs,
            out_specs=pl.BlockSpec((rows, columns), place),
        ),
        out_shape=jax.ShapeDtypeStruct((2 * rows, columns), BF),
        input_output_aliases={3: 0} if so_far is not None else {},
        cost_estimate=pl.CostEstimate(
            flops=2 * rows * columns * width, bytes_accessed=2 * columns * width, transcendentals=0
        ),
        compiler_params=params(),
        name="merge",
    )(*operands)


def add(*values):
    return sum(value.astype(F32) for value in values).astype(BF)


def ring_reduce(pieces, axis):
    own, up, down, low, high = pieces
    low, high = shift(low, axis, 1), shift(high, axis, -1)
    cut = low.shape[0]
    up = lax.dynamic_update_slice(up, add(up[:cut], low), (0,) * up.ndim)
    down = lax.dynamic_update_slice(down, add(down[cut:], high), (cut,) + (0,) * (up.ndim - 1))
    from_below, from_above = shift(up, axis, 1), shift(down, axis, -1)
    return [add(own[e], from_below[e], from_above[e]) for e in range(own.shape[0])]


def direct_reduce(pieces, axis):
    return add(pieces[0], *[shift(piece, axis, step) for step, piece in enumerate(pieces) if step])


def ring_gather(items):
    near = [[a, shift(a, axis, 1), shift(a, axis, -1)] for a, axis in items]

    def second(near):
        out = []
        for (_, axis), (_, before, after) in zip(items, near):
            cut = before.shape[0] // 2
            out.append([shift(before[:cut], axis, 1), shift(after[cut:], axis, -1)])
        return out

    return near, second


def body(deltas, sketch):
    tasks, rows, width = deltas.shape
    core, yh, yl = lax.axis_index("core"), lax.axis_index("yh"), lax.axis_index("yl")
    x, z = lax.axis_index("x"), lax.axis_index("z")
    at, core0, yh0 = lax.optimization_barrier(
        (jnp.stack([x, z, yh, core]).astype(jnp.int32), core == 0, yh == 0)
    )

    *terms, pool_keep, pool_give = sketch_call(at, deltas, sketch)
    sum0 = ring_reduce(terms[:5], "x")
    sum1 = ring_reduce(terms[5:], "z")
    pool_got = shift(pool_give, "core", 1)
    sum0 = direct_reduce(sum0, "z")
    sum1 = direct_reduce(sum1, "x")

    piece, rank = sum0.shape[1:]
    both = jnp.concatenate([sum0, sum1], axis=2).reshape(2, 2, piece, 2 * rank)
    keep = jnp.where(core0, both[:, 0], both[:, 1])
    give = jnp.where(core0, both[:, 1], both[:, 0])
    got = shift(give, "core", 1)
    chip = jnp.concatenate(
        [jnp.where(core0, keep, got), jnp.where(core0, got, keep)], axis=2
    )
    pair = add(chip, shift(chip, "yl", 1))
    across = lax.ppermute(pair, RING_Y, [(0, 3), (3, 0), (1, 2), (2, 1)])
    local = jnp.concatenate(
        [jnp.where(yh0, pair, across), jnp.where(yh0, across, pair)], axis=2
    )

    near, _ = ring_gather([(local[0][None], "x"), (local[1][None], "z")])
    half = local.shape[2] // 2
    far = [
        jnp.concatenate([shift(n[1][..., :half], axis, 1), shift(n[2][..., half:], axis, -1)], axis=2)
        for n, axis in zip(near, ("x", "z"))
    ]
    items = [(jnp.concatenate([*n, f]), axis) for n, f, axis in zip(near, far, ("z", "x"))]
    near, second = ring_gather(items)
    pooled = [add(pool_keep[i], pool_got[i]) for i in range(2)]
    near, pooled = lax.optimization_barrier((near, pooled))
    far = second(near)
    acc, basis = gram_first_call(at, near[0] + near[1])
    far, acc, basis = lax.optimization_barrier((far, acc, basis))
    gram_own, basis = gram_last_call(at, far[0] + far[1], acc, basis)
    gram_other = shift(gram_own, "core", 1)
    mine, give, chunk = coeff_call(at, basis.reshape(2, width // 4, basis.shape[-1]), pooled)
    give, gram_own, gram_other = lax.optimization_barrier((give, gram_own, gram_other))
    twin = shift(give, "core", 1)
    y, zz, frob = first_call(gram_own, gram_other)
    twin, y, zz = lax.optimization_barrier((twin, y, zz))
    chip_sum = (mine.astype(F32) + twin.astype(F32)).astype(BF)
    chip_sum, y, zz = lax.optimization_barrier((chip_sum, y, zz))
    over = shift(chip_sum, "yh", 1)
    inverse_root, chunk = rest_call(y, zz, chunk)
    over, inverse_root = lax.optimization_barrier((over, inverse_root))
    total_tasks = tasks * lax.axis_size("yh") * lax.axis_size("core")
    coeff = ((chip_sum.astype(F32) + over.astype(F32)) / total_tasks).astype(BF)

    third = third_call(coeff, inverse_root, frob)
    third_twin = shift(third, "core", 1)
    return merge_call(at, third_twin, chunk, merge_call(at, third, chunk, None))


def solution(mesh):
    fine = Mesh(mesh.devices.reshape(2, 2, 4, 2, 4), ("yh", "core", "x", "yl", "z"))
    task, row = ("yh", "core"), ("x", "yl", "z")
    return jax.shard_map(
        body,
        mesh=fine,
        in_specs=(P(task, row, None), P(row, None)),
        out_specs=P(row, task),
        check_vma=False,
    )
```

```python
import functools

import jax
import jax.numpy as jnp
from jax import lax
from jax.experimental import pallas as pl
from jax.experimental.pallas import tpu as pltpu
from jax.sharding import Mesh
from jax.sharding import PartitionSpec as P

NS_STEPS = 5
BF = jnp.bfloat16
F32 = jnp.float32
NS_BLOCK = 256
GRAM_BLOCK = 256
MIB = 1024 * 1024
RING_Y = ("yh", "yl")


def params(mib=24):
    return pltpu.CompilerParams(vmem_limit_bytes=mib * MIB)


def whole():
    return pl.BlockSpec(memory_space=pltpu.VMEM)


def shift(value, axis, step):
    size = lax.axis_size(axis)
    return lax.ppermute(value, axis, [(i, (i + step) % size) for i in range(size)])


def sketch_kernel(at_ref, deltas_ref, sketch_ref, *rest):
    outs, keep_ref, give_ref, rows_ref = rest[:10], rest[10], rest[11], rest[12]
    quarter = pl.program_id(0)
    rank = sketch_ref.shape[1]
    piece = rows_ref.shape[2]
    x, z = at_ref[0], at_ref[1]
    for task in range(2):
        part = lax.dot_general(
            sketch_ref[...], deltas_ref[task], (((0,), (0,)), ((), ())), preferred_element_type=F32
        )
        rows_ref[...] = part.astype(BF).T.reshape(4, 4, piece, rank)
        own, up, down, low, high = outs[5 * task : 5 * task + 5]
        for d in range(4):
            for e in range(4):
                over_x, over_z = (d, e) if task == 0 else (e, d)
                value = rows_ref[lax.rem(x + over_x, 4), lax.rem(z + over_z, 4)]
                if d == 2:
                    (low if e < 2 else high)[e % 2, quarter] = value
                else:
                    (own, up, None, down)[d][e, quarter] = value

    total = deltas_ref[0] + deltas_ref[1]
    mine = quarter % 2 == at_ref[3]

    @pl.when(mine)
    def _():
        keep_ref[0] = total

    @pl.when(jnp.logical_not(mine))
    def _():
        give_ref[0] = total


def sketch_call(at, deltas, sketch):
    tasks, rows, width = deltas.shape
    rank = sketch.shape[1]
    quarter = width // 4
    full, half = (4, 4, quarter // 16, rank), (2, 4, quarter // 16, rank)
    shapes = [full, full, full, half, half] * 2
    return pl.pallas_call(
        sketch_kernel,
        grid_spec=pltpu.PrefetchScalarGridSpec(
            num_scalar_prefetch=1,
            grid=(4,),
            in_specs=[
                pl.BlockSpec((tasks, rows, quarter), lambda i, at: (0, 0, i)),
                pl.BlockSpec((rows, rank), lambda i, at: (0, 0)),
            ],
            out_specs=[pl.BlockSpec(shape, lambda i, at: (0, 0, 0, 0)) for shape in shapes]
            + [pl.BlockSpec((1, rows, quarter), lambda i, at: (i // 2, 0, 0))] * 2,
            scratch_shapes=[pltpu.VMEM(full, BF)],
        ),
        out_shape=[jax.ShapeDtypeStruct(shape, BF) for shape in shapes]
        + [jax.ShapeDtypeStruct((2, rows, quarter), BF)] * 2,
        compiler_params=params(48),
        name="sketch",
    )(at, deltas, sketch)


def upper_blocks(size, block):
    return [(slice(i, i + block), slice(i, size)) for i in range(0, size, block)]


def mirror(out, rows, value, block):
    first = rows.start
    out[rows, first:] = value
    for j in range(block, value.shape[1], block):
        out[first + j : first + j + block, rows] = value[:, j : j + block].T


def pack_rows(refs, packed_ref):
    at = 0
    for ref in refs:
        count, rows, width = ref.shape
        packed_ref[at : at + count * rows, :] = ref[...].reshape(count * rows, width)
        at += count * rows


def place_rows(at_ref, blocks, basis_ref):
    x, z = at_ref[0], at_ref[1]
    for ref, chunk, outer, first in blocks:
        for j in range(ref.shape[0]):
            inner = (0, -1, 1, 2)[first + j]
            over_x, over_z = (inner, outer) if chunk == 0 else (outer, inner)
            basis_ref[chunk, lax.rem(x + over_x + 4, 4), lax.rem(z + over_z + 4, 4)] = ref[j]


def gram_first_kernel(at_ref, a0, a1, a2, b0, b1, b2, acc_ref, basis_ref, packed_ref):
    pack_rows([a0, a1, a2, b0, b1, b2], packed_ref)
    for rows, columns in upper_blocks(acc_ref.shape[0], GRAM_BLOCK):
        acc_ref[rows, columns] = lax.dot_general(
            packed_ref[:, rows], packed_ref[:, columns], (((0,), (0,)), ((), ())), preferred_element_type=F32
        )
    near = [(a0, 0, 0, 0), (a1, 0, -1, 0), (a2, 0, 1, 0), (b0, 1, 0, 0), (b1, 1, -1, 0), (b2, 1, 1, 0)]
    place_rows(at_ref, near, basis_ref)


def gram_first_call(at, parts):
    count, rows, width = parts[0].shape
    return pl.pallas_call(
        gram_first_kernel,
        in_specs=[pl.BlockSpec(memory_space=pltpu.SMEM)] + [whole()] * 6,
        out_specs=[whole()] * 2,
        out_shape=[
            jax.ShapeDtypeStruct((width, width), F32),
            jax.ShapeDtypeStruct((2, 4, 4, rows, width), BF),
        ],
        scratch_shapes=[pltpu.VMEM((6 * count * rows, width), BF)],
        cost_estimate=pl.CostEstimate(
            flops=8 * count * rows * width * width, bytes_accessed=8 * count * rows * width, transcendentals=0
        ),
        compiler_params=params(24),
        name="gram_first",
    )(at, *parts)


def gram_last_kernel(at_ref, a3, a4, b3, b4, acc_ref, near_ref, gram_ref, basis_ref, packed_ref):
    pack_rows([a3, a4, b3, b4], packed_ref)
    for rows, columns in upper_blocks(acc_ref.shape[0], GRAM_BLOCK):
        value = lax.dot_general(
            packed_ref[:, rows], packed_ref[:, columns], (((0,), (0,)), ((), ())), preferred_element_type=F32
        )
        mirror(gram_ref, rows, (acc_ref[rows, columns] + value).astype(BF), GRAM_BLOCK)
    basis_ref[...] = near_ref[...]
    place_rows(at_ref, [(a3, 0, 2, 0), (a4, 0, 2, 2), (b3, 1, 2, 0), (b4, 1, 2, 2)], basis_ref)


def gram_last_call(at, parts, acc, near):
    count, rows, width = parts[0].shape
    return pl.pallas_call(
        gram_last_kernel,
        in_specs=[pl.BlockSpec(memory_space=pltpu.SMEM)] + [whole()] * 6,
        out_specs=[whole()] * 2,
        out_shape=[
            jax.ShapeDtypeStruct((width, width), BF),
            jax.ShapeDtypeStruct(near.shape, BF),
        ],
        scratch_shapes=[pltpu.VMEM((4 * count * rows, width), BF)],
        compiler_params=params(24),
        name="gram_last",
    )(at, *parts, acc, near)


def coeff_kernel(at_ref, basis_ref, pool0_ref, pool1_ref, keep_ref, give_ref, chunk_ref):
    chunk_ref[...] = basis_ref[at_ref[2]]
    half, width = keep_ref.shape
    block = 256
    for out_ref, which in ((give_ref, 1 - at_ref[3]), (keep_ref, at_ref[3])):
        rows = pl.ds(pl.multiple_of(which * half, 16), half)
        for i in range(0, width, block):
            columns = slice(i, i + block)
            value = jnp.dot(pool0_ref[rows, :], basis_ref[0, :, columns], preferred_element_type=F32)
            value = value + jnp.dot(pool1_ref[rows, :], basis_ref[1, :, columns], preferred_element_type=F32)
            out_ref[:, columns] = value.astype(BF)


def coeff_call(at, basis, pooled):
    _, depth, width = basis.shape
    rows = pooled[0].shape[0]
    half = jax.ShapeDtypeStruct((rows // 2, width), BF)
    return pl.pallas_call(
        coeff_kernel,
        in_specs=[pl.BlockSpec(memory_space=pltpu.SMEM)] + [whole()] * 3,
        out_specs=[whole()] * 3,
        out_shape=[half, half, jax.ShapeDtypeStruct((depth, width), BF)],
        cost_estimate=pl.CostEstimate(
            flops=4 * rows * depth * width, bytes_accessed=4 * rows * depth, transcendentals=0
        ),
        compiler_params=params(20),
        name="coeff",
    )(at, basis, *pooled)


def diagonal(shape, first_row, first_col):
    row = lax.broadcasted_iota(jnp.int32, shape, 0) + first_row
    col = lax.broadcasted_iota(jnp.int32, shape, 1) + first_col
    return jnp.where(row == col, 3.0, 0.0)


def product(left, right, out, turn):
    for rows, columns in upper_blocks(left.shape[0], NS_BLOCK):
        value = jnp.dot(left[rows, :], right[:, columns], preferred_element_type=F32)
        if turn:
            value = (diagonal(value.shape, rows.start, columns.start) - value) * 0.5
        mirror(out, rows, value.astype(BF), NS_BLOCK)


def schulz_kernel(own_ref, other_ref, chunk_ref, z_ref, frob_ref, turned_ref, gram_ref, y_ref, t_ref, y2_ref, z2_ref):
    size = own_ref.shape[0]
    total = jnp.zeros((8, size), F32)
    for i in range(0, size, NS_BLOCK):
        rows = slice(i, i + NS_BLOCK)
        gram = own_ref[rows, :].astype(F32) + other_ref[rows, :].astype(F32)
        gram_ref[rows, :] = gram
        total = total + jnp.sum((gram * gram).reshape(NS_BLOCK // 8, 8, size), axis=0)
    frob = jnp.sqrt(jnp.sum(total, keepdims=True))
    frob_ref[...] = jnp.broadcast_to(frob, frob_ref.shape)
    scale = 1.0 / frob
    for i in range(0, size, NS_BLOCK):
        rows = slice(i, i + NS_BLOCK)
        y = (gram_ref[rows, :] * scale).astype(BF)
        y2_ref[rows, :] = y
        z_ref[rows, :] = ((diagonal(y.shape, i, 0) - y.astype(F32)) * 0.5).astype(BF)

    product(y2_ref, z_ref, y_ref, False)

    @pl.loop(1, NS_STEPS)
    def _(iteration):
        product(z_ref, y_ref, t_ref, True)
        product(t_ref, z_ref, z2_ref, False)
        z_ref[...] = z2_ref[...]

        @pl.when(iteration + 1 < NS_STEPS)
        def _():
            product(t_ref, y_ref, y2_ref, False)
            y_ref[...] = y2_ref[...]

    for i in range(0, chunk_ref.shape[0], NS_BLOCK):
        turned_ref[:, i : i + NS_BLOCK] = chunk_ref[i : i + NS_BLOCK, :].T


def schulz_call(own, other, chunk):
    size = own.shape[0]
    return pl.pallas_call(
        schulz_kernel,
        in_specs=[whole()] * 3,
        out_specs=[whole()] * 3,
        out_shape=[
            jax.ShapeDtypeStruct((size, size), BF),
            jax.ShapeDtypeStruct((8, 128), F32),
            jax.ShapeDtypeStruct(chunk.shape[::-1], BF),
        ],
        scratch_shapes=[pltpu.VMEM((size, size), F32)] + [pltpu.VMEM((size, size), BF)] * 4,
        cost_estimate=pl.CostEstimate(
            flops=24 * size**3, bytes_accessed=8 * size**2, transcendentals=0
        ),
        compiler_params=params(32),
        name="schulz",
    )(own, other, chunk)


def third_kernel(coeff_ref, z_ref, frob_ref, out_ref):
    second = jnp.dot(coeff_ref[...], z_ref[...], preferred_element_type=F32).astype(BF)
    third = jnp.dot(second, z_ref[...], preferred_element_type=F32)
    out_ref[...] = (third / frob_ref[0:1, 0:1]).astype(BF)


def third_call(coeff, z, frob):
    return pl.pallas_call(
        third_kernel,
        in_specs=[whole()] * 3,
        out_specs=whole(),
        out_shape=jax.ShapeDtypeStruct(coeff.shape, BF),
        compiler_params=params(),
        name="third",
    )(coeff, z, frob)


def merge_kernel(at_ref, third_ref, chunk_ref, *rest):
    out_ref = rest[-1]
    out_ref[...] = jnp.dot(third_ref[...], chunk_ref[...], preferred_element_type=F32).astype(BF)


def merge_call(at, third, chunk, so_far):
    rows, width = third.shape
    columns = chunk.shape[1]
    in_specs = [
        pl.BlockSpec((rows, width), lambda i, at: (0, 0)),
        pl.BlockSpec((width, columns), lambda i, at: (0, 0)),
    ]
    operands = [at, third, chunk]
    if so_far is None:
        place = lambda i, at: (at[3], 0)
    else:
        place = lambda i, at: (1 - at[3], 0)
        in_specs.append(pl.BlockSpec(memory_space=pl.ANY))
        operands.append(so_far)
    return pl.pallas_call(
        merge_kernel,
        grid_spec=pltpu.PrefetchScalarGridSpec(
            num_scalar_prefetch=1,
            grid=(1,),
            in_specs=in_specs,
            out_specs=pl.BlockSpec((rows, columns), place),
        ),
        out_shape=jax.ShapeDtypeStruct((2 * rows, columns), BF),
        input_output_aliases={3: 0} if so_far is not None else {},
        cost_estimate=pl.CostEstimate(
            flops=2 * rows * columns * width, bytes_accessed=2 * columns * width, transcendentals=0
        ),
        compiler_params=params(),
        name="merge",
    )(*operands)


def add(*values):
    return sum(value.astype(F32) for value in values).astype(BF)


def ring_reduce(pieces, axis):
    own, up, down, low, high = pieces
    low, high = shift(low, axis, 1), shift(high, axis, -1)
    cut = low.shape[0]
    up = lax.dynamic_update_slice(up, add(up[:cut], low), (0,) * up.ndim)
    down = lax.dynamic_update_slice(down, add(down[cut:], high), (cut,) + (0,) * (up.ndim - 1))
    from_below, from_above = shift(up, axis, 1), shift(down, axis, -1)
    return [add(own[e], from_below[e], from_above[e]) for e in range(own.shape[0])]


def direct_reduce(pieces, axis):
    return add(pieces[0], *[shift(piece, axis, step) for step, piece in enumerate(pieces) if step])


def ring_gather(items):
    near = [[a, shift(a, axis, 1), shift(a, axis, -1)] for a, axis in items]

    def second(near):
        out = []
        for (_, axis), (_, before, after) in zip(items, near):
            cut = before.shape[0] // 2
            out.append([shift(before[:cut], axis, 1), shift(after[cut:], axis, -1)])
        return out

    return near, second


def body(deltas, sketch):
    tasks, rows, width = deltas.shape
    core, yh, yl = lax.axis_index("core"), lax.axis_index("yh"), lax.axis_index("yl")
    x, z = lax.axis_index("x"), lax.axis_index("z")
    at, core0, yh0 = lax.optimization_barrier(
        (jnp.stack([x, z, yh, core]).astype(jnp.int32), core == 0, yh == 0)
    )

    *terms, pool_keep, pool_give = sketch_call(at, deltas, sketch)
    sum0 = ring_reduce(terms[:5], "x")
    sum1 = ring_reduce(terms[5:], "z")
    pool_got = shift(pool_give, "core", 1)
    sum0 = direct_reduce(sum0, "z")
    sum1 = direct_reduce(sum1, "x")

    piece, rank = sum0.shape[1:]
    both = jnp.concatenate([sum0, sum1], axis=2).reshape(2, 2, piece, 2 * rank)
    keep = jnp.where(core0, both[:, 0], both[:, 1])
    give = jnp.where(core0, both[:, 1], both[:, 0])
    got = shift(give, "core", 1)
    chip = jnp.concatenate(
        [jnp.where(core0, keep, got), jnp.where(core0, got, keep)], axis=2
    )
    pair = add(chip, shift(chip, "yl", 1))
    across = lax.ppermute(pair, RING_Y, [(0, 3), (3, 0), (1, 2), (2, 1)])
    local = jnp.concatenate(
        [jnp.where(yh0, pair, across), jnp.where(yh0, across, pair)], axis=2
    )

    near, _ = ring_gather([(local[0][None], "x"), (local[1][None], "z")])
    half = local.shape[2] // 2
    far = [
        jnp.concatenate([shift(n[1][..., :half], axis, 1), shift(n[2][..., half:], axis, -1)], axis=2)
        for n, axis in zip(near, ("x", "z"))
    ]
    items = [(jnp.concatenate([*n, f]), axis) for n, f, axis in zip(near, far, ("z", "x"))]
    near, second = ring_gather(items)
    pooled = [add(pool_keep[i], pool_got[i]) for i in range(2)]
    near, pooled = lax.optimization_barrier((near, pooled))
    far = second(near)
    acc, basis = gram_first_call(at, near[0] + near[1])
    far, acc, basis = lax.optimization_barrier((far, acc, basis))
    gram_own, basis = gram_last_call(at, far[0] + far[1], acc, basis)
    gram_other = shift(gram_own, "core", 1)
    mine, give, chunk = coeff_call(at, basis.reshape(2, width // 4, basis.shape[-1]), pooled)
    give, gram_own, gram_other = lax.optimization_barrier((give, gram_own, gram_other))
    twin = shift(give, "core", 1)
    chip_sum, gram_own, gram_other = lax.optimization_barrier((add(mine, twin), gram_own, gram_other))
    over = shift(chip_sum, "yh", 1)
    inverse_root, frob, chunk = schulz_call(gram_own, gram_other, chunk)
    over, inverse_root = lax.optimization_barrier((over, inverse_root))
    total_tasks = tasks * lax.axis_size("yh") * lax.axis_size("core")
    coeff = ((chip_sum.astype(F32) + over.astype(F32)) / total_tasks).astype(BF)

    third = third_call(coeff, inverse_root, frob)
    third_twin = shift(third, "core", 1)
    return merge_call(at, third_twin, chunk, merge_call(at, third, chunk, None))


def solution(mesh):
    fine = Mesh(mesh.devices.reshape(2, 2, 4, 2, 4), ("yh", "core", "x", "yl", "z"))
    task, row = ("yh", "core"), ("x", "yl", "z")
    return jax.shard_map(
        body,
        mesh=fine,
        in_specs=(P(task, row, None), P(row, None)),
        out_specs=P(row, task),
        check_vma=False,
    )
```

```python
import functools

import jax
import jax.numpy as jnp
from jax import lax
from jax.experimental import pallas as pl
from jax.experimental.pallas import tpu as pltpu
from jax.sharding import Mesh
from jax.sharding import PartitionSpec as P

NS_STEPS = 5
BF = jnp.bfloat16
F32 = jnp.float32
NS_BLOCK = 256
GRAM_BLOCK = 256
MERGE_BLOCK = 256
FETCH_AHEAD = 2
MIB = 1024 * 1024
RING_Y = ("yh", "yl")


def params(mib=24):
    return pltpu.CompilerParams(vmem_limit_bytes=mib * MIB)


def whole():
    return pl.BlockSpec(memory_space=pltpu.VMEM)


def shift(value, axis, step):
    size = lax.axis_size(axis)
    return lax.ppermute(value, axis, [(i, (i + step) % size) for i in range(size)])


def halving_order(at, index):
    near = at + 1 - 2 * lax.rem(at, 2)
    return (at, 3 - at, near, 3 - near)[index]


def sketch_kernel(at_ref, deltas_any, sketch_ref, *rest):
    outs, keep_any, give_any = rest[:10], rest[10], rest[11]
    rows_ref, held_ref, pool_ref, in_sem, out_sem = rest[12:]
    quarters, tasks, rows, quarter = held_ref.shape
    rank = sketch_ref.shape[1]
    piece = rows_ref.shape[2]
    x, z = at_ref[0], at_ref[1]

    def fetch(q, task):
        columns = pl.ds(pl.multiple_of(q * quarter, quarter), quarter)
        return pltpu.make_async_copy(deltas_any.at[task, :, columns], held_ref.at[q, task], in_sem.at[q, task])

    for q in range(FETCH_AHEAD):
        for task in range(tasks):
            fetch(q, task).start()

    @pl.loop(0, quarters)
    def _(q):
        for task in range(tasks):
            fetch(q, task).wait()

            @pl.when(q + FETCH_AHEAD < quarters)
            def _():
                fetch(q + FETCH_AHEAD, task).start()

            part = lax.dot_general(
                sketch_ref[...], held_ref[q, task], (((0,), (0,)), ((), ())), preferred_element_type=F32
            )
            rows_ref[...] = part.astype(BF).T.reshape(4, 4, piece, rank)
            own, up, down, low, high = outs[5 * task : 5 * task + 5]
            for d in range(4):
                for e in range(4):
                    if task == 0:
                        value = rows_ref[lax.rem(x + d, 4), halving_order(z, e)]
                    else:
                        value = rows_ref[halving_order(x, e), lax.rem(z + d, 4)]
                    if d == 2:
                        (low if e < 2 else high)[e % 2, q] = value
                    else:
                        (own, up, None, down)[d][e, q] = value
        pool_ref[q] = held_ref[q, 0] + held_ref[q, 1]
        mine = at_ref[3] == lax.rem(q, 2)
        for target, wanted in ((keep_any, mine), (give_any, jnp.logical_not(mine))):

            @pl.when(wanted)
            def _(target=target):
                pltpu.make_async_copy(pool_ref.at[q], target.at[q // 2], out_sem.at[q]).start()

    for q in range(quarters):
        pltpu.make_async_copy(pool_ref.at[q], keep_any.at[q // 2], out_sem.at[q]).wait()


def sketch_call(at, deltas, sketch):
    tasks, rows, width = deltas.shape
    rank = sketch.shape[1]
    quarter = width // 4
    full, half = (4, 4, quarter // 16, rank), (2, 4, quarter // 16, rank)
    shapes = [full, full, full, half, half] * 2
    anywhere = pl.BlockSpec(memory_space=pl.ANY)
    return pl.pallas_call(
        sketch_kernel,
        in_specs=[pl.BlockSpec(memory_space=pltpu.SMEM), anywhere, whole()],
        out_specs=[whole()] * len(shapes) + [anywhere] * 2,
        out_shape=[jax.ShapeDtypeStruct(shape, BF) for shape in shapes]
        + [jax.ShapeDtypeStruct((2, rows, quarter), BF)] * 2,
        scratch_shapes=[
            pltpu.VMEM(full, BF),
            pltpu.VMEM((4, tasks, rows, quarter), BF),
            pltpu.VMEM((4, rows, quarter), BF),
            pltpu.SemaphoreType.DMA((4, tasks)),
            pltpu.SemaphoreType.DMA((4,)),
        ],
        compiler_params=params(48),
        name="sketch",
    )(at, deltas, sketch)


def upper_blocks(size, block):
    return [(slice(i, i + block), slice(i, size)) for i in range(0, size, block)]


def mirror(out, rows, value, block):
    first = rows.start
    out[rows, first:] = value
    for j in range(block, value.shape[1], block):
        out[first + j : first + j + block, rows] = value[:, j : j + block].T


def pack_rows(refs, packed_ref):
    at = 0
    for ref in refs:
        count, rows, width = ref.shape
        packed_ref[at : at + count * rows, :] = ref[...].reshape(count * rows, width)
        at += count * rows


def place_rows(at_ref, blocks, basis_ref):
    x, z = at_ref[0], at_ref[1]
    for ref, chunk, outer, first in blocks:
        for j in range(ref.shape[0]):
            inner = (0, -1, 1, 2)[first + j]
            over_x, over_z = (inner, outer) if chunk == 0 else (outer, inner)
            basis_ref[chunk, lax.rem(x + over_x + 4, 4), lax.rem(z + over_z + 4, 4)] = ref[j]


def gram_first_kernel(at_ref, a0, a1, a2, b0, b1, b2, acc_ref, basis_ref, packed_ref):
    pack_rows([a0, a1, a2, b0, b1, b2], packed_ref)
    for rows, columns in upper_blocks(acc_ref.shape[0], GRAM_BLOCK):
        acc_ref[rows, columns] = lax.dot_general(
            packed_ref[:, rows], packed_ref[:, columns], (((0,), (0,)), ((), ())), preferred_element_type=F32
        )
    near = [(a0, 0, 0, 0), (a1, 0, -1, 0), (a2, 0, 1, 0), (b0, 1, 0, 0), (b1, 1, -1, 0), (b2, 1, 1, 0)]
    place_rows(at_ref, near, basis_ref)


def gram_first_call(at, parts):
    count, rows, width = parts[0].shape
    return pl.pallas_call(
        gram_first_kernel,
        in_specs=[pl.BlockSpec(memory_space=pltpu.SMEM)] + [whole()] * 6,
        out_specs=[whole()] * 2,
        out_shape=[
            jax.ShapeDtypeStruct((width, width), F32),
            jax.ShapeDtypeStruct((2, 4, 4, rows, width), BF),
        ],
        scratch_shapes=[pltpu.VMEM((6 * count * rows, width), BF)],
        cost_estimate=pl.CostEstimate(
            flops=8 * count * rows * width * width, bytes_accessed=8 * count * rows * width, transcendentals=0
        ),
        compiler_params=params(24),
        name="gram_first",
    )(at, *parts)


def gram_last_kernel(at_ref, a3, a4, b3, b4, acc_ref, near_ref, gram_ref, basis_ref, packed_ref):
    pack_rows([a3, a4, b3, b4], packed_ref)
    for rows, columns in upper_blocks(acc_ref.shape[0], GRAM_BLOCK):
        value = lax.dot_general(
            packed_ref[:, rows], packed_ref[:, columns], (((0,), (0,)), ((), ())), preferred_element_type=F32
        )
        mirror(gram_ref, rows, (acc_ref[rows, columns] + value).astype(BF), GRAM_BLOCK)
    basis_ref[...] = near_ref[...]
    place_rows(at_ref, [(a3, 0, 2, 0), (a4, 0, 2, 2), (b3, 1, 2, 0), (b4, 1, 2, 2)], basis_ref)


def gram_last_call(at, parts, acc, near):
    count, rows, width = parts[0].shape
    return pl.pallas_call(
        gram_last_kernel,
        in_specs=[pl.BlockSpec(memory_space=pltpu.SMEM)] + [whole()] * 6,
        out_specs=[whole()] * 2,
        out_shape=[
            jax.ShapeDtypeStruct((width, width), BF),
            jax.ShapeDtypeStruct(near.shape, BF),
        ],
        scratch_shapes=[pltpu.VMEM((4 * count * rows, width), BF)],
        compiler_params=params(24),
        name="gram_last",
    )(at, *parts, acc, near)


def coeff_kernel(at_ref, basis_ref, pool0_ref, pool1_ref, out_ref, *, own):
    half, width = out_ref.shape
    which = at_ref[3] if own else 1 - at_ref[3]
    block = 256
    rows = pl.ds(pl.multiple_of(which * half, 16), half)
    for i in range(0, width, block):
        columns = slice(i, i + block)
        value = jnp.dot(pool0_ref[rows, :], basis_ref[0, :, columns], preferred_element_type=F32)
        value = value + jnp.dot(pool1_ref[rows, :], basis_ref[1, :, columns], preferred_element_type=F32)
        out_ref[:, columns] = value.astype(BF)


def coeff_call(at, basis, pooled, own):
    _, depth, width = basis.shape
    rows = pooled[0].shape[0]
    return pl.pallas_call(
        functools.partial(coeff_kernel, own=own),
        in_specs=[pl.BlockSpec(memory_space=pltpu.SMEM)] + [whole()] * 3,
        out_specs=whole(),
        out_shape=jax.ShapeDtypeStruct((rows // 2, width), BF),
        cost_estimate=pl.CostEstimate(
            flops=2 * rows * depth * width, bytes_accessed=4 * rows * depth, transcendentals=0
        ),
        compiler_params=params(20),
        name="coeff",
    )(at, basis, *pooled)


def diagonal(shape, first_row, first_col):
    row = lax.broadcasted_iota(jnp.int32, shape, 0) + first_row
    col = lax.broadcasted_iota(jnp.int32, shape, 1) + first_col
    return jnp.where(row == col, 3.0, 0.0)


def product(left, right, out, turn):
    for rows, columns in upper_blocks(left.shape[0], NS_BLOCK):
        value = jnp.dot(left[rows, :], right[:, columns], preferred_element_type=F32)
        if turn:
            value = (diagonal(value.shape, rows.start, columns.start) - value) * 0.5
        mirror(out, rows, value.astype(BF), NS_BLOCK)


def schulz_kernel(own_ref, other_ref, z_ref, frob_ref, gram_ref, y_ref, t_ref, y2_ref, z2_ref):
    size = own_ref.shape[0]
    total = jnp.zeros((8, size), F32)
    for i in range(0, size, NS_BLOCK):
        rows = slice(i, i + NS_BLOCK)
        gram = own_ref[rows, :].astype(F32) + other_ref[rows, :].astype(F32)
        gram_ref[rows, :] = gram
        total = total + jnp.sum((gram * gram).reshape(NS_BLOCK // 8, 8, size), axis=0)
    frob = jnp.sqrt(jnp.sum(total, keepdims=True))
    frob_ref[...] = jnp.broadcast_to(frob, frob_ref.shape)
    scale = 1.0 / frob
    for i in range(0, size, NS_BLOCK):
        rows = slice(i, i + NS_BLOCK)
        y = (gram_ref[rows, :] * scale).astype(BF)
        y2_ref[rows, :] = y
        z_ref[rows, :] = ((diagonal(y.shape, i, 0) - y.astype(F32)) * 0.5).astype(BF)

    product(y2_ref, z_ref, y_ref, False)

    @pl.loop(1, NS_STEPS)
    def _(iteration):
        product(z_ref, y_ref, t_ref, True)
        product(t_ref, z_ref, z2_ref, False)
        z_ref[...] = z2_ref[...]

        @pl.when(iteration + 1 < NS_STEPS)
        def _():
            product(t_ref, y_ref, y2_ref, False)
            y_ref[...] = y2_ref[...]


def schulz_call(own, other):
    size = own.shape[0]
    return pl.pallas_call(
        schulz_kernel,
        in_specs=[whole()] * 2,
        out_specs=[whole()] * 2,
        out_shape=[
            jax.ShapeDtypeStruct((size, size), BF),
            jax.ShapeDtypeStruct((8, 128), F32),
        ],
        scratch_shapes=[pltpu.VMEM((size, size), F32)] + [pltpu.VMEM((size, size), BF)] * 4,
        cost_estimate=pl.CostEstimate(
            flops=24 * size**3, bytes_accessed=8 * size**2, transcendentals=0
        ),
        compiler_params=params(32),
        name="schulz",
    )(own, other)


def third_kernel(chip_ref, over_ref, z_ref, frob_ref, out_ref, *, tasks):
    coeff = ((chip_ref[...].astype(F32) + over_ref[...].astype(F32)) / tasks).astype(BF)
    second = jnp.dot(coeff, z_ref[...], preferred_element_type=F32).astype(BF)
    third = jnp.dot(second, z_ref[...], preferred_element_type=F32)
    out_ref[...] = (third / frob_ref[0:1, 0:1]).astype(BF)


def third_call(chip_sum, over, z, frob, tasks):
    return pl.pallas_call(
        functools.partial(third_kernel, tasks=tasks),
        in_specs=[whole()] * 4,
        out_specs=whole(),
        out_shape=jax.ShapeDtypeStruct(chip_sum.shape, BF),
        compiler_params=params(),
        name="third",
    )(chip_sum, over, z, frob)


def merge_own_kernel(at_ref, third_ref, chunk_ref, out_any, turned_ref, stage_ref, sem):
    merge_rows(at_ref, at_ref[3], third_ref, turned_ref, out_any, stage_ref, sem, chunk_ref)


def merge_twin_kernel(at_ref, third_ref, turned_ref, so_far_any, out_any, stage_ref, sem):
    merge_rows(at_ref, 1 - at_ref[3], third_ref, turned_ref, out_any, stage_ref, sem)


def merge_rows(at_ref, which, third_ref, turned_ref, out_any, stage_ref, sem, chunk_ref=None):
    half, width = stage_ref.shape
    rows = pl.ds(pl.multiple_of(which * half, 16), half)
    copies = []
    for i in range(0, width, MERGE_BLOCK):
        columns = slice(i, i + MERGE_BLOCK)
        if chunk_ref is not None:
            turned_ref[:, columns] = chunk_ref[at_ref[2], columns, :].T
        stage_ref[:, columns] = jnp.dot(
            third_ref[...], turned_ref[:, columns], preferred_element_type=F32
        ).astype(BF)
        target = out_any.at[rows, pl.ds(i, MERGE_BLOCK)]
        copies.append(pltpu.make_async_copy(stage_ref.at[:, columns], target, sem.at[len(copies)]))
        copies[-1].start()
    for copy in copies:
        copy.wait()


def merge_call(at, third, chunk, so_far=None):
    rows, width = third.shape
    first = so_far is None
    columns = chunk.shape[1]
    anywhere = pl.BlockSpec(memory_space=pl.ANY)
    merged = jax.ShapeDtypeStruct((2 * rows, columns), BF)
    turned = jax.ShapeDtypeStruct((width, columns), BF)
    return pl.pallas_call(
        merge_own_kernel if first else merge_twin_kernel,
        in_specs=[pl.BlockSpec(memory_space=pltpu.SMEM), whole(), whole()] + ([] if first else [anywhere]),
        out_specs=[anywhere, whole()] if first else anywhere,
        out_shape=[merged, turned] if first else merged,
        input_output_aliases={} if first else {3: 0},
        scratch_shapes=[
            pltpu.VMEM((rows, columns), BF),
            pltpu.SemaphoreType.DMA((columns // MERGE_BLOCK,)),
        ],
        cost_estimate=pl.CostEstimate(
            flops=2 * rows * columns * width, bytes_accessed=2 * columns * width, transcendentals=0
        ),
        compiler_params=params(),
        name="merge",
    )(at, third, chunk, *([] if first else [so_far]))


def add(*values):
    return sum(value.astype(F32) for value in values).astype(BF)


def ring_reduce(pieces, axis):
    own, up, down, low, high = pieces
    low, high = shift(low, axis, 1), shift(high, axis, -1)
    cut = low.shape[0]
    up = lax.dynamic_update_slice(up, add(up[:cut], low), (0,) * up.ndim)
    down = lax.dynamic_update_slice(down, add(down[cut:], high), (cut,) + (0,) * (up.ndim - 1))
    from_below, from_above = shift(up, axis, 1), shift(down, axis, -1)
    half = own.shape[0] // 2
    keep = [add(own[e], from_below[e], from_above[e]) for e in range(half)]
    give = add(own[half:], from_below[half:], from_above[half:])
    return keep, give


def halving_reduce(keep, give, axis):
    got = lax.ppermute(give, axis, [(0, 1), (1, 0), (2, 3), (3, 2)])
    mine, other = add(keep[0], got[0]), add(keep[1], got[1])
    return add(mine, lax.ppermute(other, axis, [(0, 3), (3, 0), (1, 2), (2, 1)]))


def ring_gather(items):
    near = [[a, shift(a, axis, 1), shift(a, axis, -1)] for a, axis in items]

    def second(near):
        out = []
        for (_, axis), (_, before, after) in zip(items, near):
            cut = before.shape[0] // 2
            out.append([shift(before[:cut], axis, 1), shift(after[cut:], axis, -1)])
        return out

    return near, second


def body(deltas, sketch):
    tasks, rows, width = deltas.shape
    core, yh, yl = lax.axis_index("core"), lax.axis_index("yh"), lax.axis_index("yl")
    x, z = lax.axis_index("x"), lax.axis_index("z")
    at, core0, yh0, yl0 = lax.optimization_barrier(
        (jnp.stack([x, z, yh, core]).astype(jnp.int32), core == 0, yh == 0, yl == 0)
    )

    *terms, pool_keep, pool_give = sketch_call(at, deltas, sketch)
    sum0 = ring_reduce(terms[:5], "x")
    sum1 = ring_reduce(terms[5:], "z")
    pool_got = shift(pool_give, "core", 1)
    sum0 = halving_reduce(*sum0, "z")
    sum1 = halving_reduce(*sum1, "x")

    piece, rank = sum0.shape[1:]
    both = jnp.concatenate([sum0, sum1], axis=2).reshape(2, 2, piece, 2 * rank)
    keep = jnp.where(core0, both[:, 0], both[:, 1])
    give = jnp.where(core0, both[:, 1], both[:, 0])
    got = shift(give, "core", 1)
    chip = jnp.concatenate(
        [jnp.where(core0, keep, got), jnp.where(core0, got, keep)], axis=2
    )
    below, above, across = [shift(chip, RING_Y, step) for step in (1, -1, 2)]
    ours = add(chip, jnp.where(yl0, above, below))
    theirs = add(across, jnp.where(yl0, below, above))
    local = jnp.concatenate([jnp.where(yh0, ours, theirs), jnp.where(yh0, theirs, ours)], axis=2)

    near, _ = ring_gather([(local[0][None], "x"), (local[1][None], "z")])
    half = local.shape[2] // 2
    far = [
        jnp.concatenate([shift(n[1][..., :half], axis, 1), shift(n[2][..., half:], axis, -1)], axis=2)
        for n, axis in zip(near, ("x", "z"))
    ]
    items = [(jnp.concatenate([*n, f]), axis) for n, f, axis in zip(near, far, ("z", "x"))]
    near, second = ring_gather(items)
    pooled = [add(pool_keep[i], pool_got[i]) for i in range(2)]
    near, pooled = lax.optimization_barrier((near, pooled))
    far = second(near)
    acc, basis = gram_first_call(at, near[0] + near[1])
    far, acc, basis = lax.optimization_barrier((far, acc, basis))
    gram_own, basis = gram_last_call(at, far[0] + far[1], acc, basis)
    gram_other = shift(gram_own, "core", 1)
    basis = basis.reshape(2, width // 4, basis.shape[-1])
    give = coeff_call(at, basis, pooled, False)
    give, pooled = lax.optimization_barrier((give, pooled))
    twin = shift(give, "core", 1)
    mine = coeff_call(at, basis, pooled, True)
    twin, mine, gram_own, gram_other = lax.optimization_barrier((twin, mine, gram_own, gram_other))
    chip_sum, gram_own, gram_other = lax.optimization_barrier((add(mine, twin), gram_own, gram_other))
    over = shift(chip_sum, "yh", 1)
    inverse_root, frob = schulz_call(gram_own, gram_other)
    over, inverse_root = lax.optimization_barrier((over, inverse_root))
    total_tasks = tasks * lax.axis_size("yh") * lax.axis_size("core")
    third = third_call(chip_sum, over, inverse_root, frob, total_tasks)
    third_twin = shift(third, "core", 1)
    merged, turned = merge_call(at, third, basis)
    return merge_call(at, third_twin, turned, merged)


def solution(mesh):
    fine = Mesh(mesh.devices.reshape(2, 2, 4, 2, 4), ("yh", "core", "x", "yl", "z"))
    task, row = ("yh", "core"), ("x", "yl", "z")
    return jax.shard_map(
        body,
        mesh=fine,
        in_specs=(P(task, row, None), P(row, None)),
        out_specs=P(row, task),
        check_vma=False,
    )
```

```python
import functools

import jax
import jax.numpy as jnp
from jax import lax
from jax.experimental import pallas as pl
from jax.experimental.pallas import tpu as pltpu
from jax.sharding import Mesh
from jax.sharding import PartitionSpec as P

NS_STEPS = 5
BF = jnp.bfloat16
F32 = jnp.float32
NS_BLOCK = 256
GRAM_BLOCK = 256
MERGE_BLOCK = 256
FETCH_AHEAD = 2
MIB = 1024 * 1024
RING_Y = ("yh", "yl")


def params(mib=24):
    return pltpu.CompilerParams(vmem_limit_bytes=mib * MIB)


def whole():
    return pl.BlockSpec(memory_space=pltpu.VMEM)


def shift(value, axis, step):
    size = lax.axis_size(axis)
    return lax.ppermute(value, axis, [(i, (i + step) % size) for i in range(size)])


def halving_order(at, index):
    near = at + 1 - 2 * lax.rem(at, 2)
    return (at, 3 - at, near, 3 - near)[index]


def sketch_kernel(at_ref, deltas_any, sketch_ref, *rest):
    outs, keep_any, give_any = rest[:10], rest[10], rest[11]
    rows_ref, held_ref, pool_ref, in_sem, out_sem = rest[12:]
    quarters, tasks, rows, quarter = held_ref.shape
    rank = sketch_ref.shape[1]
    piece = rows_ref.shape[2]
    x, z = at_ref[0], at_ref[1]

    def fetch(q, task):
        columns = pl.ds(pl.multiple_of(q * quarter, quarter), quarter)
        return pltpu.make_async_copy(deltas_any.at[task, :, columns], held_ref.at[q, task], in_sem.at[q, task])

    for q in range(FETCH_AHEAD):
        for task in range(tasks):
            fetch(q, task).start()

    @pl.loop(0, quarters)
    def _(q):
        for task in range(tasks):
            fetch(q, task).wait()

            @pl.when(q + FETCH_AHEAD < quarters)
            def _():
                fetch(q + FETCH_AHEAD, task).start()

            part = lax.dot_general(
                sketch_ref[...], held_ref[q, task], (((0,), (0,)), ((), ())), preferred_element_type=F32
            )
            rows_ref[...] = part.astype(BF).T.reshape(4, 4, piece, rank)
            own, up, down, low, high = outs[5 * task : 5 * task + 5]
            for d in range(4):
                for e in range(4):
                    if task == 0:
                        value = rows_ref[lax.rem(x + d, 4), halving_order(z, e)]
                    else:
                        value = rows_ref[halving_order(x, e), lax.rem(z + d, 4)]
                    if d == 2:
                        (low if e < 2 else high)[e % 2, q] = value
                    else:
                        (own, up, None, down)[d][e, q] = value
        pool_ref[q] = held_ref[q, 0] + held_ref[q, 1]
        mine = at_ref[3] == lax.rem(q, 2)
        for target, wanted in ((keep_any, mine), (give_any, jnp.logical_not(mine))):

            @pl.when(wanted)
            def _(target=target):
                pltpu.make_async_copy(pool_ref.at[q], target.at[q // 2], out_sem.at[q]).start()

    for q in range(quarters):
        pltpu.make_async_copy(pool_ref.at[q], keep_any.at[q // 2], out_sem.at[q]).wait()


def sketch_call(at, deltas, sketch):
    tasks, rows, width = deltas.shape
    rank = sketch.shape[1]
    quarter = width // 4
    full, half = (4, 4, quarter // 16, rank), (2, 4, quarter // 16, rank)
    shapes = [full, full, full, half, half] * 2
    anywhere = pl.BlockSpec(memory_space=pl.ANY)
    return pl.pallas_call(
        sketch_kernel,
        in_specs=[pl.BlockSpec(memory_space=pltpu.SMEM), anywhere, whole()],
        out_specs=[whole()] * len(shapes) + [anywhere] * 2,
        out_shape=[jax.ShapeDtypeStruct(shape, BF) for shape in shapes]
        + [jax.ShapeDtypeStruct((2, rows, quarter), BF)] * 2,
        scratch_shapes=[
            pltpu.VMEM(full, BF),
            pltpu.VMEM((4, tasks, rows, quarter), BF),
            pltpu.VMEM((4, rows, quarter), BF),
            pltpu.SemaphoreType.DMA((4, tasks)),
            pltpu.SemaphoreType.DMA((4,)),
        ],
        compiler_params=params(48),
        name="sketch",
    )(at, deltas, sketch)


def upper_blocks(size, block):
    return [(slice(i, i + block), slice(i, size)) for i in range(0, size, block)]


def mirror(out, rows, value, block):
    first = rows.start
    out[rows, first:] = value
    for j in range(block, value.shape[1], block):
        out[first + j : first + j + block, rows] = value[:, j : j + block].T


def pack_rows(refs, packed_ref):
    at = 0
    for ref in refs:
        count, rows, width = ref.shape
        packed_ref[at : at + count * rows, :] = ref[...].reshape(count * rows, width)
        at += count * rows


def place_rows(at_ref, blocks, basis_ref):
    x, z = at_ref[0], at_ref[1]
    for ref, chunk, outer, first in blocks:
        for j in range(ref.shape[0]):
            inner = (0, -1, 1, 2)[first + j]
            over_x, over_z = (inner, outer) if chunk == 0 else (outer, inner)
            basis_ref[chunk, lax.rem(x + over_x + 4, 4), lax.rem(z + over_z + 4, 4)] = ref[j]


def gram_first_kernel(at_ref, a0, a1, a2, b0, b1, b2, acc_ref, basis_ref, packed_ref):
    pack_rows([a0, a1, a2, b0, b1, b2], packed_ref)
    for rows, columns in upper_blocks(acc_ref.shape[0], GRAM_BLOCK):
        acc_ref[rows, columns] = lax.dot_general(
            packed_ref[:, rows], packed_ref[:, columns], (((0,), (0,)), ((), ())), preferred_element_type=F32
        )
    near = [(a0, 0, 0, 0), (a1, 0, -1, 0), (a2, 0, 1, 0), (b0, 1, 0, 0), (b1, 1, -1, 0), (b2, 1, 1, 0)]
    place_rows(at_ref, near, basis_ref)


def gram_first_call(at, parts):
    count, rows, width = parts[0].shape
    return pl.pallas_call(
        gram_first_kernel,
        in_specs=[pl.BlockSpec(memory_space=pltpu.SMEM)] + [whole()] * 6,
        out_specs=[whole()] * 2,
        out_shape=[
            jax.ShapeDtypeStruct((width, width), F32),
            jax.ShapeDtypeStruct((2, 4, 4, rows, width), BF),
        ],
        scratch_shapes=[pltpu.VMEM((6 * count * rows, width), BF)],
        cost_estimate=pl.CostEstimate(
            flops=8 * count * rows * width * width, bytes_accessed=8 * count * rows * width, transcendentals=0
        ),
        compiler_params=params(24),
        name="gram_first",
    )(at, *parts)


def gram_last_kernel(at_ref, a3, a4, b3, b4, acc_ref, near_ref, gram_ref, basis_ref, packed_ref):
    pack_rows([a3, a4, b3, b4], packed_ref)
    for rows, columns in upper_blocks(acc_ref.shape[0], GRAM_BLOCK):
        value = lax.dot_general(
            packed_ref[:, rows], packed_ref[:, columns], (((0,), (0,)), ((), ())), preferred_element_type=F32
        )
        mirror(gram_ref, rows, (acc_ref[rows, columns] + value).astype(BF), GRAM_BLOCK)
    basis_ref[...] = near_ref[...]
    place_rows(at_ref, [(a3, 0, 2, 0), (a4, 0, 2, 2), (b3, 1, 2, 0), (b4, 1, 2, 2)], basis_ref)


def gram_last_call(at, parts, acc, near):
    count, rows, width = parts[0].shape
    return pl.pallas_call(
        gram_last_kernel,
        in_specs=[pl.BlockSpec(memory_space=pltpu.SMEM)] + [whole()] * 6,
        out_specs=[whole()] * 2,
        out_shape=[
            jax.ShapeDtypeStruct((width, width), BF),
            jax.ShapeDtypeStruct(near.shape, BF),
        ],
        scratch_shapes=[pltpu.VMEM((4 * count * rows, width), BF)],
        compiler_params=params(24),
        name="gram_last",
    )(at, *parts, acc, near)


def coeff_kernel(at_ref, basis_ref, pool0_ref, pool1_ref, out_ref, *, own):
    half, width = out_ref.shape
    which = at_ref[3] if own else 1 - at_ref[3]
    block = 256
    rows = pl.ds(pl.multiple_of(which * half, 16), half)
    for i in range(0, width, block):
        columns = slice(i, i + block)
        value = jnp.dot(pool0_ref[rows, :], basis_ref[0, :, columns], preferred_element_type=F32)
        value = value + jnp.dot(pool1_ref[rows, :], basis_ref[1, :, columns], preferred_element_type=F32)
        out_ref[:, columns] = value.astype(BF)


def coeff_call(at, basis, pooled, own):
    _, depth, width = basis.shape
    rows = pooled[0].shape[0]
    return pl.pallas_call(
        functools.partial(coeff_kernel, own=own),
        in_specs=[pl.BlockSpec(memory_space=pltpu.SMEM)] + [whole()] * 3,
        out_specs=whole(),
        out_shape=jax.ShapeDtypeStruct((rows // 2, width), BF),
        cost_estimate=pl.CostEstimate(
            flops=2 * rows * depth * width, bytes_accessed=4 * rows * depth, transcendentals=0
        ),
        compiler_params=params(20),
        name="coeff",
    )(at, basis, *pooled)


def diagonal(shape, first_row, first_col):
    row = lax.broadcasted_iota(jnp.int32, shape, 0) + first_row
    col = lax.broadcasted_iota(jnp.int32, shape, 1) + first_col
    return jnp.where(row == col, 3.0, 0.0)


def product(left, right, out, turn):
    for rows, columns in upper_blocks(left.shape[0], NS_BLOCK):
        value = jnp.dot(left[rows, :], right[:, columns], preferred_element_type=F32)
        if turn:
            value = (diagonal(value.shape, rows.start, columns.start) - value) * 0.5
        mirror(out, rows, value.astype(BF), NS_BLOCK)


def schulz_kernel(own_ref, other_ref, z_ref, frob_ref, gram_ref, y_ref, t_ref, y2_ref, z2_ref):
    size = own_ref.shape[0]
    total = jnp.zeros((8, size), F32)
    for i in range(0, size, NS_BLOCK):
        rows = slice(i, i + NS_BLOCK)
        gram = own_ref[rows, :].astype(F32) + other_ref[rows, :].astype(F32)
        gram_ref[rows, :] = gram
        total = total + jnp.sum((gram * gram).reshape(NS_BLOCK // 8, 8, size), axis=0)
    frob = jnp.sqrt(jnp.sum(total, keepdims=True))
    frob_ref[...] = jnp.broadcast_to(frob, frob_ref.shape)
    scale = 1.0 / frob
    for i in range(0, size, NS_BLOCK):
        rows = slice(i, i + NS_BLOCK)
        y = (gram_ref[rows, :] * scale).astype(BF)
        y2_ref[rows, :] = y
        z_ref[rows, :] = ((diagonal(y.shape, i, 0) - y.astype(F32)) * 0.5).astype(BF)

    product(y2_ref, z_ref, y_ref, False)

    @pl.loop(1, NS_STEPS)
    def _(iteration):
        product(z_ref, y_ref, t_ref, True)
        product(t_ref, z_ref, z2_ref, False)
        z_ref[...] = z2_ref[...]

        @pl.when(iteration + 1 < NS_STEPS)
        def _():
            product(t_ref, y_ref, y2_ref, False)
            y_ref[...] = y2_ref[...]


def schulz_call(own, other):
    size = own.shape[0]
    return pl.pallas_call(
        schulz_kernel,
        in_specs=[whole()] * 2,
        out_specs=[whole()] * 2,
        out_shape=[
            jax.ShapeDtypeStruct((size, size), BF),
            jax.ShapeDtypeStruct((8, 128), F32),
        ],
        scratch_shapes=[pltpu.VMEM((size, size), F32)] + [pltpu.VMEM((size, size), BF)] * 4,
        cost_estimate=pl.CostEstimate(
            flops=24 * size**3, bytes_accessed=8 * size**2, transcendentals=0
        ),
        compiler_params=params(32),
        name="schulz",
    )(own, other)


def third_kernel(chip_ref, over_ref, z_ref, frob_ref, out_ref, *, tasks):
    coeff = ((chip_ref[...].astype(F32) + over_ref[...].astype(F32)) / tasks).astype(BF)
    second = jnp.dot(coeff, z_ref[...], preferred_element_type=F32).astype(BF)
    third = jnp.dot(second, z_ref[...], preferred_element_type=F32)
    out_ref[...] = (third / frob_ref[0:1, 0:1]).astype(BF)


def third_call(chip_sum, over, z, frob, tasks):
    return pl.pallas_call(
        functools.partial(third_kernel, tasks=tasks),
        in_specs=[whole()] * 4,
        out_specs=whole(),
        out_shape=jax.ShapeDtypeStruct(chip_sum.shape, BF),
        compiler_params=params(),
        name="third",
    )(chip_sum, over, z, frob)


def merge_own_kernel(at_ref, third_ref, basis_ref, out_ref, turned_ref):
    for i in range(0, out_ref.shape[1], MERGE_BLOCK):
        columns = slice(i, i + MERGE_BLOCK)
        turned_ref[:, columns] = basis_ref[at_ref[2], columns, :].T
        out_ref[:, columns] = jnp.dot(
            third_ref[...], turned_ref[:, columns], preferred_element_type=F32
        ).astype(BF)


def merge_own_call(at, third, basis):
    rows, width = third.shape
    columns = basis.shape[1]
    return pl.pallas_call(
        merge_own_kernel,
        in_specs=[pl.BlockSpec(memory_space=pltpu.SMEM), whole(), whole()],
        out_specs=[whole(), whole()],
        out_shape=[jax.ShapeDtypeStruct((rows, columns), BF), jax.ShapeDtypeStruct((width, columns), BF)],
        cost_estimate=pl.CostEstimate(
            flops=2 * rows * columns * width, bytes_accessed=2 * columns * width, transcendentals=0
        ),
        compiler_params=params(),
        name="merge_own",
    )(at, third, basis)


def merge_kernel(at_ref, third_ref, turned_ref, own_ref, out_any, twin_ref, sem):
    half, width = own_ref.shape
    own_rows = pl.ds(pl.multiple_of(at_ref[3] * half, 16), half)
    twin_rows = pl.ds(pl.multiple_of((1 - at_ref[3]) * half, 16), half)
    copies = [pltpu.make_async_copy(own_ref, out_any.at[own_rows, :], sem.at[0])]
    copies[0].start()
    for i in range(0, width, MERGE_BLOCK):
        columns = slice(i, i + MERGE_BLOCK)
        twin_ref[:, columns] = jnp.dot(
            third_ref[...], turned_ref[:, columns], preferred_element_type=F32
        ).astype(BF)
        target = out_any.at[twin_rows, pl.ds(i, MERGE_BLOCK)]
        copies.append(pltpu.make_async_copy(twin_ref.at[:, columns], target, sem.at[len(copies)]))
        copies[-1].start()
    for copy in copies:
        copy.wait()


def merge_call(at, third, turned, own):
    rows, columns = own.shape
    return pl.pallas_call(
        merge_kernel,
        in_specs=[pl.BlockSpec(memory_space=pltpu.SMEM)] + [whole()] * 3,
        out_specs=pl.BlockSpec(memory_space=pl.ANY),
        out_shape=jax.ShapeDtypeStruct((2 * rows, columns), BF),
        scratch_shapes=[
            pltpu.VMEM((rows, columns), BF),
            pltpu.SemaphoreType.DMA((1 + columns // MERGE_BLOCK,)),
        ],
        compiler_params=params(),
        name="merge",
    )(at, third, turned, own)


def add(*values):
    return sum(value.astype(F32) for value in values).astype(BF)


def ring_reduce(pieces, axis):
    own, up, down, low, high = pieces
    low, high = shift(low, axis, 1), shift(high, axis, -1)
    cut = low.shape[0]
    up = lax.dynamic_update_slice(up, add(up[:cut], low), (0,) * up.ndim)
    down = lax.dynamic_update_slice(down, add(down[cut:], high), (cut,) + (0,) * (up.ndim - 1))
    from_below, from_above = shift(up, axis, 1), shift(down, axis, -1)
    half = own.shape[0] // 2
    keep = [add(own[e], from_below[e], from_above[e]) for e in range(half)]
    give = add(own[half:], from_below[half:], from_above[half:])
    return keep, give


def halving_reduce(keep, give, axis):
    got = lax.ppermute(give, axis, [(0, 1), (1, 0), (2, 3), (3, 2)])
    mine, other = add(keep[0], got[0]), add(keep[1], got[1])
    return add(mine, lax.ppermute(other, axis, [(0, 3), (3, 0), (1, 2), (2, 1)]))


def ring_gather(items):
    near = [[a, shift(a, axis, 1), shift(a, axis, -1)] for a, axis in items]

    def second(near):
        out = []
        for (_, axis), (_, before, after) in zip(items, near):
            cut = before.shape[0] // 2
            out.append([shift(before[:cut], axis, 1), shift(after[cut:], axis, -1)])
        return out

    return near, second


def body(deltas, sketch):
    tasks, rows, width = deltas.shape
    core, yh, yl = lax.axis_index("core"), lax.axis_index("yh"), lax.axis_index("yl")
    x, z = lax.axis_index("x"), lax.axis_index("z")
    at, core0, yh0, yl0 = lax.optimization_barrier(
        (jnp.stack([x, z, yh, core]).astype(jnp.int32), core == 0, yh == 0, yl == 0)
    )

    *terms, pool_keep, pool_give = sketch_call(at, deltas, sketch)
    sum0 = ring_reduce(terms[:5], "x")
    sum1 = ring_reduce(terms[5:], "z")
    pool_got = shift(pool_give, "core", 1)
    sum0 = halving_reduce(*sum0, "z")
    sum1 = halving_reduce(*sum1, "x")

    piece, rank = sum0.shape[1:]
    both = jnp.concatenate([sum0, sum1], axis=2).reshape(2, 2, piece, 2 * rank)
    keep = jnp.where(core0, both[:, 0], both[:, 1])
    give = jnp.where(core0, both[:, 1], both[:, 0])
    got = shift(give, "core", 1)
    chip = jnp.concatenate(
        [jnp.where(core0, keep, got), jnp.where(core0, got, keep)], axis=2
    )
    pooled = [add(pool_keep[i], pool_got[i]) for i in range(2)]
    (below, above, across), pooled = lax.optimization_barrier(
        ([shift(chip, RING_Y, step) for step in (1, -1, 2)], pooled)
    )
    ours = add(chip, jnp.where(yl0, above, below))
    theirs = add(across, jnp.where(yl0, below, above))
    local = jnp.concatenate([jnp.where(yh0, ours, theirs), jnp.where(yh0, theirs, ours)], axis=2)

    near, _ = ring_gather([(local[0][None], "x"), (local[1][None], "z")])
    half = local.shape[2] // 2
    far = [
        jnp.concatenate([shift(n[1][..., :half], axis, 1), shift(n[2][..., half:], axis, -1)], axis=2)
        for n, axis in zip(near, ("x", "z"))
    ]
    items = [(jnp.concatenate([*n, f]), axis) for n, f, axis in zip(near, far, ("z", "x"))]
    near, second = ring_gather(items)
    far = second(near)
    acc, basis = gram_first_call(at, near[0] + near[1])
    far, acc, basis = lax.optimization_barrier((far, acc, basis))
    gram_own, basis = gram_last_call(at, far[0] + far[1], acc, basis)
    gram_other = shift(gram_own, "core", 1)
    basis = basis.reshape(2, width // 4, basis.shape[-1])
    give = coeff_call(at, basis, pooled, False)
    give, pooled = lax.optimization_barrier((give, pooled))
    twin = shift(give, "core", 1)
    mine = coeff_call(at, basis, pooled, True)
    twin, mine, gram_own, gram_other = lax.optimization_barrier((twin, mine, gram_own, gram_other))
    chip_sum, gram_own, gram_other = lax.optimization_barrier((add(mine, twin), gram_own, gram_other))
    over = shift(chip_sum, "yh", 1)
    inverse_root, frob = schulz_call(gram_own, gram_other)
    over, inverse_root = lax.optimization_barrier((over, inverse_root))
    total_tasks = tasks * lax.axis_size("yh") * lax.axis_size("core")
    third = third_call(chip_sum, over, inverse_root, frob, total_tasks)
    third_twin = shift(third, "core", 1)
    merged, turned = merge_own_call(at, third, basis)
    return merge_call(at, third_twin, turned, merged)


def solution(mesh):
    fine = Mesh(mesh.devices.reshape(2, 2, 4, 2, 4), ("yh", "core", "x", "yl", "z"))
    task, row = ("yh", "core"), ("x", "yl", "z")
    return jax.shard_map(
        body,
        mesh=fine,
        in_specs=(P(task, row, None), P(row, None)),
        out_specs=P(row, task),
        check_vma=False,
    )
```

```python
import functools

import jax
import jax.numpy as jnp
from jax import lax
from jax.experimental import pallas as pl
from jax.experimental.pallas import tpu as pltpu
from jax.sharding import Mesh
from jax.sharding import PartitionSpec as P

NS_STEPS = 5
BF = jnp.bfloat16
F32 = jnp.float32
NS_BLOCK = 256
GRAM_BLOCK = 256
MERGE_BLOCK = 256
FETCH_AHEAD = 2
MIB = 1024 * 1024
RING_Y = ("yh", "yl")


def params(mib=24):
    return pltpu.CompilerParams(vmem_limit_bytes=mib * MIB)


def whole():
    return pl.BlockSpec(memory_space=pltpu.VMEM)


def shift(value, axis, step):
    size = lax.axis_size(axis)
    return lax.ppermute(value, axis, [(i, (i + step) % size) for i in range(size)])


def halving_order(at, index):
    near = at + 1 - 2 * lax.rem(at, 2)
    return (at, 3 - at, near, 3 - near)[index]


def sketch_kernel(at_ref, deltas_any, sketch_ref, *rest):
    outs, keep_any, give_any = rest[:10], rest[10], rest[11]
    rows_ref, held_ref, pool_ref, in_sem, out_sem = rest[12:]
    quarters, tasks, rows, quarter = held_ref.shape
    rank = sketch_ref.shape[1]
    piece = rows_ref.shape[2]
    x, z = at_ref[0], at_ref[1]

    def fetch(q, task):
        columns = pl.ds(pl.multiple_of(q * quarter, quarter), quarter)
        return pltpu.make_async_copy(deltas_any.at[task, :, columns], held_ref.at[q, task], in_sem.at[q, task])

    for q in range(FETCH_AHEAD):
        for task in range(tasks):
            fetch(q, task).start()

    @pl.loop(0, quarters)
    def _(q):
        for task in range(tasks):
            fetch(q, task).wait()

            @pl.when(q + FETCH_AHEAD < quarters)
            def _():
                fetch(q + FETCH_AHEAD, task).start()

            part = lax.dot_general(
                sketch_ref[...], held_ref[q, task], (((0,), (0,)), ((), ())), preferred_element_type=F32
            )
            rows_ref[...] = part.astype(BF).T.reshape(4, 4, piece, rank)
            own, up, down, low, high = outs[5 * task : 5 * task + 5]
            for d in range(4):
                for e in range(4):
                    if task == 0:
                        value = rows_ref[lax.rem(x + d, 4), halving_order(z, e)]
                    else:
                        value = rows_ref[halving_order(x, e), lax.rem(z + d, 4)]
                    if d == 2:
                        (low if e < 2 else high)[e % 2, q] = value
                    else:
                        (own, up, None, down)[d][e, q] = value
        pool_ref[q] = held_ref[q, 0] + held_ref[q, 1]
        mine = at_ref[3] == lax.rem(q, 2)
        for target, wanted in ((keep_any, mine), (give_any, jnp.logical_not(mine))):

            @pl.when(wanted)
            def _(target=target):
                pltpu.make_async_copy(pool_ref.at[q], target.at[q // 2], out_sem.at[q]).start()

    for q in range(quarters):
        pltpu.make_async_copy(pool_ref.at[q], keep_any.at[q // 2], out_sem.at[q]).wait()


def sketch_call(at, deltas, sketch):
    tasks, rows, width = deltas.shape
    rank = sketch.shape[1]
    quarter = width // 4
    full, half = (4, 4, quarter // 16, rank), (2, 4, quarter // 16, rank)
    shapes = [full, full, full, half, half] * 2
    anywhere = pl.BlockSpec(memory_space=pl.ANY)
    return pl.pallas_call(
        sketch_kernel,
        in_specs=[pl.BlockSpec(memory_space=pltpu.SMEM), anywhere, whole()],
        out_specs=[whole()] * len(shapes) + [anywhere] * 2,
        out_shape=[jax.ShapeDtypeStruct(shape, BF) for shape in shapes]
        + [jax.ShapeDtypeStruct((2, rows, quarter), BF)] * 2,
        scratch_shapes=[
            pltpu.VMEM(full, BF),
            pltpu.VMEM((4, tasks, rows, quarter), BF),
            pltpu.VMEM((4, rows, quarter), BF),
            pltpu.SemaphoreType.DMA((4, tasks)),
            pltpu.SemaphoreType.DMA((4,)),
        ],
        compiler_params=params(48),
        name="sketch",
    )(at, deltas, sketch)


def upper_blocks(size, block):
    return [(slice(i, i + block), slice(i, size)) for i in range(0, size, block)]


def mirror(out, rows, value, block):
    first = rows.start
    out[rows, first:] = value
    for j in range(block, value.shape[1], block):
        out[first + j : first + j + block, rows] = value[:, j : j + block].T


def pack_rows(refs, packed_ref):
    at = 0
    for ref in refs:
        count, rows, width = ref.shape
        packed_ref[at : at + count * rows, :] = ref[...].reshape(count * rows, width)
        at += count * rows


def place_rows(at_ref, blocks, basis_ref):
    x, z = at_ref[0], at_ref[1]
    for ref, chunk, outer, first in blocks:
        for j in range(ref.shape[0]):
            inner = (0, -1, 1, 2)[first + j]
            over_x, over_z = (inner, outer) if chunk == 0 else (outer, inner)
            basis_ref[lax.rem(x + over_x + 4, 4), lax.rem(z + over_z + 4, 4)] = ref[j]


def gram_first_kernel(at_ref, a0, a1, a2, b0, b1, b2, acc_ref, near_a, near_b, packed_ref):
    pack_rows([a0, a1, a2, b0, b1, b2], packed_ref)
    for rows, columns in upper_blocks(acc_ref.shape[0], GRAM_BLOCK):
        acc_ref[rows, columns] = lax.dot_general(
            packed_ref[:, rows], packed_ref[:, columns], (((0,), (0,)), ((), ())), preferred_element_type=F32
        )
    place_rows(at_ref, [(a0, 0, 0, 0), (a1, 0, -1, 0), (a2, 0, 1, 0)], near_a)
    place_rows(at_ref, [(b0, 1, 0, 0), (b1, 1, -1, 0), (b2, 1, 1, 0)], near_b)


def gram_first_call(at, parts):
    count, rows, width = parts[0].shape
    return pl.pallas_call(
        gram_first_kernel,
        in_specs=[pl.BlockSpec(memory_space=pltpu.SMEM)] + [whole()] * 6,
        out_specs=[whole()] * 3,
        out_shape=[
            jax.ShapeDtypeStruct((width, width), F32),
            jax.ShapeDtypeStruct((4, 4, rows, width), BF),
            jax.ShapeDtypeStruct((4, 4, rows, width), BF),
        ],
        scratch_shapes=[pltpu.VMEM((6 * count * rows, width), BF)],
        cost_estimate=pl.CostEstimate(
            flops=8 * count * rows * width * width, bytes_accessed=8 * count * rows * width, transcendentals=0
        ),
        compiler_params=params(24),
        name="gram_first",
    )(at, *parts)


def gram_more_kernel(at_ref, low, high, acc_ref, near_ref, out_ref, basis_ref, packed_ref, *, chunk):
    pack_rows([low, high], packed_ref)
    for rows, columns in upper_blocks(acc_ref.shape[0], GRAM_BLOCK):
        value = acc_ref[rows, columns] + lax.dot_general(
            packed_ref[:, rows], packed_ref[:, columns], (((0,), (0,)), ((), ())), preferred_element_type=F32
        )
        if chunk == 0:
            out_ref[rows, columns] = value
        else:
            mirror(out_ref, rows, value.astype(BF), GRAM_BLOCK)
    basis_ref[...] = near_ref[...]
    place_rows(at_ref, [(low, chunk, 2, 0), (high, chunk, 2, 2)], basis_ref)


def gram_more_call(at, parts, acc, near, chunk):
    count, rows, width = parts[0].shape
    return pl.pallas_call(
        functools.partial(gram_more_kernel, chunk=chunk),
        in_specs=[pl.BlockSpec(memory_space=pltpu.SMEM)] + [whole()] * 4,
        out_specs=[whole()] * 2,
        out_shape=[
            jax.ShapeDtypeStruct((width, width), BF if chunk else F32),
            jax.ShapeDtypeStruct(near.shape, BF),
        ],
        scratch_shapes=[pltpu.VMEM((2 * count * rows, width), BF)],
        cost_estimate=pl.CostEstimate(
            flops=3 * count * rows * width * width, bytes_accessed=8 * width * width, transcendentals=0
        ),
        compiler_params=params(24),
        name="gram_more",
    )(at, *parts, acc, near)


def coeff_kernel(at_ref, basis0_ref, basis1_ref, pool0_ref, pool1_ref, out_ref, *, own):
    half, width = out_ref.shape
    which = at_ref[3] if own else 1 - at_ref[3]
    block = 256
    rows = pl.ds(pl.multiple_of(which * half, 16), half)
    for i in range(0, width, block):
        columns = slice(i, i + block)
        value = jnp.dot(pool0_ref[rows, :], basis0_ref[:, columns], preferred_element_type=F32)
        value = value + jnp.dot(pool1_ref[rows, :], basis1_ref[:, columns], preferred_element_type=F32)
        out_ref[:, columns] = value.astype(BF)


def coeff_call(at, basis, pooled, own):
    depth, width = basis[0].shape
    rows = pooled[0].shape[0]
    return pl.pallas_call(
        functools.partial(coeff_kernel, own=own),
        in_specs=[pl.BlockSpec(memory_space=pltpu.SMEM)] + [whole()] * 4,
        out_specs=whole(),
        out_shape=jax.ShapeDtypeStruct((rows // 2, width), BF),
        cost_estimate=pl.CostEstimate(
            flops=2 * rows * depth * width, bytes_accessed=4 * rows * depth, transcendentals=0
        ),
        compiler_params=params(20),
        name="coeff",
    )(at, *basis, *pooled)


def diagonal(shape, first_row, first_col):
    row = lax.broadcasted_iota(jnp.int32, shape, 0) + first_row
    col = lax.broadcasted_iota(jnp.int32, shape, 1) + first_col
    return jnp.where(row == col, 3.0, 0.0)


def product(left, right, out, turn):
    for rows, columns in upper_blocks(left.shape[0], NS_BLOCK):
        value = jnp.dot(left[rows, :], right[:, columns], preferred_element_type=F32)
        if turn:
            value = (diagonal(value.shape, rows.start, columns.start) - value) * 0.5
        mirror(out, rows, value.astype(BF), NS_BLOCK)


def schulz_kernel(own_ref, other_ref, z_ref, frob_ref, gram_ref, y_ref, t_ref, y2_ref, z2_ref):
    size = own_ref.shape[0]
    total = jnp.zeros((8, size), F32)
    for i in range(0, size, NS_BLOCK):
        rows = slice(i, i + NS_BLOCK)
        gram = own_ref[rows, :].astype(F32) + other_ref[rows, :].astype(F32)
        gram_ref[rows, :] = gram
        total = total + jnp.sum((gram * gram).reshape(NS_BLOCK // 8, 8, size), axis=0)
    frob = jnp.sqrt(jnp.sum(total, keepdims=True))
    frob_ref[...] = jnp.broadcast_to(frob, frob_ref.shape)
    scale = 1.0 / frob
    for i in range(0, size, NS_BLOCK):
        rows = slice(i, i + NS_BLOCK)
        y = (gram_ref[rows, :] * scale).astype(BF)
        y2_ref[rows, :] = y
        z_ref[rows, :] = ((diagonal(y.shape, i, 0) - y.astype(F32)) * 0.5).astype(BF)

    product(y2_ref, z_ref, y_ref, False)

    @pl.loop(1, NS_STEPS)
    def _(iteration):
        product(z_ref, y_ref, t_ref, True)
        product(t_ref, z_ref, z2_ref, False)
        z_ref[...] = z2_ref[...]

        @pl.when(iteration + 1 < NS_STEPS)
        def _():
            product(t_ref, y_ref, y2_ref, False)
            y_ref[...] = y2_ref[...]


def schulz_call(own, other):
    size = own.shape[0]
    return pl.pallas_call(
        schulz_kernel,
        in_specs=[whole()] * 2,
        out_specs=[whole()] * 2,
        out_shape=[
            jax.ShapeDtypeStruct((size, size), BF),
            jax.ShapeDtypeStruct((8, 128), F32),
        ],
        scratch_shapes=[pltpu.VMEM((size, size), F32)] + [pltpu.VMEM((size, size), BF)] * 4,
        cost_estimate=pl.CostEstimate(
            flops=24 * size**3, bytes_accessed=8 * size**2, transcendentals=0
        ),
        compiler_params=params(32),
        name="schulz",
    )(own, other)


def third_kernel(chip_ref, over_ref, z_ref, frob_ref, out_ref, *, tasks):
    coeff = ((chip_ref[...].astype(F32) + over_ref[...].astype(F32)) / tasks).astype(BF)
    second = jnp.dot(coeff, z_ref[...], preferred_element_type=F32).astype(BF)
    third = jnp.dot(second, z_ref[...], preferred_element_type=F32)
    out_ref[...] = (third / frob_ref[0:1, 0:1]).astype(BF)


def third_call(chip_sum, over, z, frob, tasks):
    return pl.pallas_call(
        functools.partial(third_kernel, tasks=tasks),
        in_specs=[whole()] * 4,
        out_specs=whole(),
        out_shape=jax.ShapeDtypeStruct(chip_sum.shape, BF),
        compiler_params=params(),
        name="third",
    )(chip_sum, over, z, frob)


def merge_own_kernel(at_ref, third_ref, basis0_ref, basis1_ref, out_ref, turned_ref):
    for i in range(0, out_ref.shape[1], MERGE_BLOCK):
        columns = slice(i, i + MERGE_BLOCK)
        chunk = jnp.where(at_ref[2] == 0, basis0_ref[columns, :], basis1_ref[columns, :])
        turned_ref[:, columns] = chunk.T
        out_ref[:, columns] = jnp.dot(
            third_ref[...], turned_ref[:, columns], preferred_element_type=F32
        ).astype(BF)


def merge_own_call(at, third, basis):
    rows, width = third.shape
    columns = basis[0].shape[0]
    return pl.pallas_call(
        merge_own_kernel,
        in_specs=[pl.BlockSpec(memory_space=pltpu.SMEM), whole(), whole(), whole()],
        out_specs=[whole(), whole()],
        out_shape=[jax.ShapeDtypeStruct((rows, columns), BF), jax.ShapeDtypeStruct((width, columns), BF)],
        cost_estimate=pl.CostEstimate(
            flops=2 * rows * columns * width, bytes_accessed=2 * columns * width, transcendentals=0
        ),
        compiler_params=params(),
        name="merge_own",
    )(at, third, *basis)


def merge_kernel(at_ref, third_ref, turned_ref, own_ref, out_any, twin_ref, sem):
    half, width = own_ref.shape
    own_rows = pl.ds(pl.multiple_of(at_ref[3] * half, 16), half)
    twin_rows = pl.ds(pl.multiple_of((1 - at_ref[3]) * half, 16), half)
    copies = [pltpu.make_async_copy(own_ref, out_any.at[own_rows, :], sem.at[0])]
    copies[0].start()
    for i in range(0, width, MERGE_BLOCK):
        columns = slice(i, i + MERGE_BLOCK)
        twin_ref[:, columns] = jnp.dot(
            third_ref[...], turned_ref[:, columns], preferred_element_type=F32
        ).astype(BF)
        target = out_any.at[twin_rows, pl.ds(i, MERGE_BLOCK)]
        copies.append(pltpu.make_async_copy(twin_ref.at[:, columns], target, sem.at[len(copies)]))
        copies[-1].start()
    for copy in copies:
        copy.wait()


def merge_call(at, third, turned, own):
    rows, columns = own.shape
    return pl.pallas_call(
        merge_kernel,
        in_specs=[pl.BlockSpec(memory_space=pltpu.SMEM)] + [whole()] * 3,
        out_specs=pl.BlockSpec(memory_space=pl.ANY),
        out_shape=jax.ShapeDtypeStruct((2 * rows, columns), BF),
        scratch_shapes=[
            pltpu.VMEM((rows, columns), BF),
            pltpu.SemaphoreType.DMA((1 + columns // MERGE_BLOCK,)),
        ],
        compiler_params=params(),
        name="merge",
    )(at, third, turned, own)


def add(*values):
    return sum(value.astype(F32) for value in values).astype(BF)


def ring_reduce(pieces, axis):
    own, up, down, low, high = pieces
    low, high = shift(low, axis, 1), shift(high, axis, -1)
    cut = low.shape[0]
    up = lax.dynamic_update_slice(up, add(up[:cut], low), (0,) * up.ndim)
    down = lax.dynamic_update_slice(down, add(down[cut:], high), (cut,) + (0,) * (up.ndim - 1))
    from_below, from_above = shift(up, axis, 1), shift(down, axis, -1)
    half = own.shape[0] // 2
    keep = [add(own[e], from_below[e], from_above[e]) for e in range(half)]
    give = add(own[half:], from_below[half:], from_above[half:])
    return keep, give


def halving_reduce(keep, give, axis):
    got = lax.ppermute(give, axis, [(0, 1), (1, 0), (2, 3), (3, 2)])
    mine, other = add(keep[0], got[0]), add(keep[1], got[1])
    return add(mine, lax.ppermute(other, axis, [(0, 3), (3, 0), (1, 2), (2, 1)]))


def ring_gather(items):
    near = [[a, shift(a, axis, 1), shift(a, axis, -1)] for a, axis in items]

    def second(near):
        out = []
        for (_, axis), (_, before, after) in zip(items, near):
            cut = before.shape[0] // 2
            out.append([shift(before[:cut], axis, 1), shift(after[cut:], axis, -1)])
        return out

    return near, second


def body(deltas, sketch):
    tasks, rows, width = deltas.shape
    core, yh, yl = lax.axis_index("core"), lax.axis_index("yh"), lax.axis_index("yl")
    x, z = lax.axis_index("x"), lax.axis_index("z")
    at, core0, yh0, yl0 = lax.optimization_barrier(
        (jnp.stack([x, z, yh, core]).astype(jnp.int32), core == 0, yh == 0, yl == 0)
    )

    *terms, pool_keep, pool_give = sketch_call(at, deltas, sketch)
    sum0 = ring_reduce(terms[:5], "x")
    sum1 = ring_reduce(terms[5:], "z")
    pool_got = shift(pool_give, "core", 1)
    sum0 = halving_reduce(*sum0, "z")
    sum1 = halving_reduce(*sum1, "x")

    piece, rank = sum0.shape[1:]
    both = jnp.concatenate([sum0, sum1], axis=2).reshape(2, 2, piece, 2 * rank)
    keep = jnp.where(core0, both[:, 0], both[:, 1])
    give = jnp.where(core0, both[:, 1], both[:, 0])
    got = shift(give, "core", 1)
    chip = jnp.concatenate(
        [jnp.where(core0, keep, got), jnp.where(core0, got, keep)], axis=2
    )
    pooled = [add(pool_keep[i], pool_got[i]) for i in range(2)]
    (below, above, across), pooled = lax.optimization_barrier(
        ([shift(chip, RING_Y, step) for step in (1, -1, 2)], pooled)
    )
    ours = add(chip, jnp.where(yl0, above, below))
    theirs = add(across, jnp.where(yl0, below, above))
    local = jnp.concatenate([jnp.where(yh0, ours, theirs), jnp.where(yh0, theirs, ours)], axis=2)

    near, _ = ring_gather([(local[0][None], "x"), (local[1][None], "z")])
    half = local.shape[2] // 2
    far = [
        jnp.concatenate([shift(n[1][..., :half], axis, 1), shift(n[2][..., half:], axis, -1)], axis=2)
        for n, axis in zip(near, ("x", "z"))
    ]
    items = [(jnp.concatenate([*n, f]), axis) for n, f, axis in zip(near, far, ("z", "x"))]
    near, second = ring_gather(items)
    far = second(near)
    acc, near_a, near_b = gram_first_call(at, near[0] + near[1])
    acc, basis_a = gram_more_call(at, far[0], acc, near_a, 0)
    gram_own, basis_b = gram_more_call(at, far[1], acc, near_b, 1)
    gram_other = shift(gram_own, "core", 1)
    basis = [part.reshape(width // 4, part.shape[-1]) for part in (basis_a, basis_b)]
    give = coeff_call(at, basis, pooled, False)
    give, pooled = lax.optimization_barrier((give, pooled))
    twin = shift(give, "core", 1)
    mine = coeff_call(at, basis, pooled, True)
    twin, mine, gram_own, gram_other = lax.optimization_barrier((twin, mine, gram_own, gram_other))
    chip_sum, gram_own, gram_other = lax.optimization_barrier((add(mine, twin), gram_own, gram_other))
    over = shift(chip_sum, "yh", 1)
    inverse_root, frob = schulz_call(gram_own, gram_other)
    over, inverse_root = lax.optimization_barrier((over, inverse_root))
    total_tasks = tasks * lax.axis_size("yh") * lax.axis_size("core")
    third = third_call(chip_sum, over, inverse_root, frob, total_tasks)
    third_twin = shift(third, "core", 1)
    merged, turned = merge_own_call(at, third, basis)
    return merge_call(at, third_twin, turned, merged)


def solution(mesh):
    fine = Mesh(mesh.devices.reshape(2, 2, 4, 2, 4), ("yh", "core", "x", "yl", "z"))
    task, row = ("yh", "core"), ("x", "yl", "z")
    return jax.shard_map(
        body,
        mesh=fine,
        in_specs=(P(task, row, None), P(row, None)),
        out_specs=P(row, task),
        check_vma=False,
    )
```
